256 devices in a mesh: view: 64 (over y, x, z_hi, core), bin: 4 (over z_lo).
Axes of the slice: x: 4, y: 4, z: 8 (z_hi: 2, z_lo: 4; z = z_hi * 4 + z_lo), core: 2. Of those that a mesh axis runs over, the one named last changes fastest.
Arguments:
- volume: bfloat16 [64, 3, 16, 256], P('view'), may hold values from -6 to 6
- basis: bfloat16 [16, 256, 128], replicated, may hold values from -0.046875 to 0.046875
- tile_index: int32 [256, 12, 56], P('view'), may hold values from 0 to 63, as said below
- tile_offset: int32 [256, 12, 56], P('view'), may hold values from 0 to 15
- attenuation: float32 [8, 3], P('bin'), may hold values from 0.1 to 0.6
- flux: float32 [8], P('bin'), may hold values from 4 to 40
- counts: int32 [256, 8, 16, 1536], P('view', 'bin'), may hold values from 0 to 63
Outputs:
- gradient: float32 [64, 3, 16, 256], P('view')
The draws below stay inside these ranges and needn't reach their ends.
Inputs may be any that keep to these rules, and one draw needn't show every extreme that they name: `tile_index`: each view's detector tile lists 56 different volume tiles.
All inputs are finite; a program needn't handle non-finite values.
Results may differ from the reference program's by a relative error of at most 0.00058.
Values may be sent and summed in bfloat16 or wider, within the bound.
No kernel may reach another device: no remote copies, remote signals or barrier semaphores. Data moves between devices by JAX's collectives and lax.ppermute only.
A program may use at most 64 MiB of HBM per device.

```python
import math
import jax
import jax.numpy as jnp
from jax import lax

M = 3
SL = 16
TV = 256
TD = 128
DET = 1536
NB = 8
NT = 64
K = 56
P_SIZE = 16
VIEWS = 256
NDT = 12


def draw_tile_index(key, part):
    key = jax.random.fold_in(key, 7)
    keys = jax.random.split(key, VIEWS * NDT)

    def pick(single):
        return jax.random.permutation(single, NT)[:K]
    lists = jax.vmap(pick)(keys)
    return lists.reshape(VIEWS, NDT, K).astype(jnp.int32)


def touch_ends(array, key, low, high):
    longest = array.shape.index(max(array.shape))
    spots = []
    for shift in (0, 1):
        where = [jax.random.randint(jax.random.fold_in(key, axis), (), 0, length) for axis, length in enumerate(array.shape)]
        where[longest] = (where[longest] + shift) % array.shape[longest]
        spots.append(tuple(where))
    return array.at[spots[0]].set(low).at[spots[1]].set(high)


def steps_of(key, shape, cuts, low, top_value):
    def one(position, parts):
        heights = jax.random.uniform(jax.random.fold_in(jax.random.fold_in(key, 6), position), (parts,), jnp.float32, low / len(cuts), top_value / len(cuts))
        return jnp.repeat(jnp.exp(heights), shape[position] // parts).reshape((-1,) + (1,) * (len(shape) - position - 1))

    factor_of = one(*cuts[0])
    for cut in cuts[1:]:
        factor_of = factor_of * one(*cut)
    return factor_of


def normal_values(stream_key, extent, spread, most, pieces=(), dtype=jnp.bfloat16):
    entries = spread * jax.random.normal(stream_key, extent, jnp.float32)
    if pieces:
        entries = entries * steps_of(stream_key, extent, pieces, -0.22, 0.18)
    return jnp.clip(entries, -most, most).astype(dtype)


def setup_inputs(seed: int = 0) -> dict:
    key_of = jax.random.split(jax.random.key(seed), 8)
    volume = normal_values(key_of[0], (NT, M, SL, TV), 1.0, 6.0, ((0, 64),))
    basis = normal_values(key_of[1], (P_SIZE, TV, TD), (K * TV) ** -0.5, 0.046875)
    tile_index = draw_tile_index(jax.random.fold_in(key_of[7], 71), 0)
    tile_offset = touch_ends(jax.random.randint(key_of[3], (VIEWS, NDT, K), 0, P_SIZE), jax.random.fold_in(key_of[3], 1), 0, P_SIZE - 1).astype(jnp.int32)
    attenuation = jnp.clip(jnp.exp(math.log(0.6) - 1.7917595 * jax.random.uniform(key_of[4], (NB, M), jnp.float32) ** steps_of(key_of[4], (NB, M), ((0, 4),), -0.2, 0.2)), 0.1, 0.6)
    flux = jnp.clip(jnp.exp(math.log(40.0) - 2.3025851 * jax.random.uniform(key_of[5], (NB,), jnp.float32) ** steps_of(key_of[5], (NB,), ((0, 4),), -0.2, 0.2)), 4.0, 40.0)
    counts = touch_ends(jax.random.randint(key_of[6], (VIEWS, NB, SL, DET), 0, 64), jax.random.fold_in(key_of[6], 1), 0, 63).astype(jnp.int32)
    return {"volume": volume, "basis": basis, "tile_index": tile_index, "tile_offset": tile_offset, "attenuation": attenuation, "flux": flux, "counts": counts}


def reference(volume, basis, tile_index, tile_offset, attenuation, flux, counts):
    channels = M * SL
    flat = volume.reshape(NT, channels, TV)
    scale = 1.0 / (8.0 * (VIEWS ** 0.5))

    def one_view(total, inputs):
        indices, offsets, photons = inputs
        tiles = jnp.take(flat, indices, axis=0).astype(jnp.float32)
        blocks = jnp.take(basis, offsets, axis=0).astype(jnp.float32)
        lines = jnp.einsum("dkcs,dkst->cdt", tiles, blocks).reshape(M, SL, DET)
        exponent = attenuation[:, 0, None, None] * lines[0][None]
        for material in range(1, M):
            exponent = exponent + attenuation[:, material, None, None] * lines[material][None]
        predicted = flux[:, None, None] * jnp.exp(-exponent)
        misfit = photons.astype(jnp.float32) - predicted
        line_grad = jnp.sum(attenuation.T[:, :, None, None] * misfit[None], axis=1)
        rounded = lax.optimization_barrier(line_grad.astype(jnp.bfloat16)).astype(jnp.float32)
        rounded = rounded.reshape(channels, NDT, TD)
        products = jnp.einsum("cdt,dkst->dkcs", rounded, blocks)
        total = total.at[indices.reshape(-1)].add(products.reshape(NDT * K, channels, TV))
        return total, None

    start = jnp.zeros((NT, channels, TV), jnp.float32)
    total, unused = lax.scan(one_view, start, (tile_index, tile_offset, counts))
    return (total * scale).reshape(NT, M, SL, TV)
```

```python
import math

import jax
import jax.numpy as jnp
from jax import lax
from jax.experimental import pallas as pl
from jax.experimental.pallas import tpu as pltpu
from jax.sharding import PartitionSpec as P

BOTH = ("view", "bin")
BF16 = jnp.bfloat16
F32 = jnp.float32

CORE = 4
FAR = 8 + 2
PLANE = 15
LINE = 11

HALF = 32
SPOTS = 16
QUARTERS = 4
CHANNELS = 12
PAIRS = 48
BANK = 16
WIDTH = 256
DEPTH = 128
SPAN = QUARTERS * DEPTH
BLOCK = 2 * CHANNELS


def partners(mask):
    return [(place, place ^ mask) for place in range(256)]


def groups_of(same):
    return [[place for place in range(256) if place & same == rest] for rest in range(256) if rest & same == rest]


def split(value):
    high = value.astype(BF16)
    low = (value - high.astype(F32)).astype(BF16)
    return high, low


def select_kernel(index_ref, offset_ref, picks_ref, places_ref):
    labels = lax.broadcasted_iota(jnp.int32, (2 * HALF, 128), 0)
    chosen = jnp.full((2 * HALF, 128), -1, jnp.int32)
    for step in range(index_ref.shape[0]):
        chosen = jnp.where(labels == index_ref[step : step + 1, :], offset_ref[step : step + 1, :], chosen)
    chosen = chosen.astype(F32)
    part = (lax.broadcasted_iota(jnp.int32, (PAIRS, 128), 1) // HALF).astype(F32)
    for core in range(2):
        mine = chosen[core * HALF : (core + 1) * HALF]
        turned = jnp.concatenate([mine] * 4, axis=0).T[:PAIRS] - part
        for j in range(BANK // 4):
            picks_ref[core, :, j * 128 : (j + 1) * 128] = (turned == 4 * j).astype(F32).astype(BF16)
        for p in range(BANK):
            places_ref[core, p * HALF : (p + 1) * HALF, :] = (mine == p).astype(F32).astype(BF16)


def select(index, offset):
    vmem = pl.BlockSpec(memory_space=pltpu.VMEM)
    return pl.pallas_call(
        select_kernel,
        out_shape=[
            jax.ShapeDtypeStruct((2, PAIRS, BANK * HALF), BF16),
            jax.ShapeDtypeStruct((2, BANK * HALF, 128), BF16),
        ],
        in_specs=[vmem] * 2,
        out_specs=[vmem] * 2,
    )(index, offset)


def project(core, volume_ref, basis_ref, picks_ref, rows_ref, high_ref, low_ref):
    rows_ref[...] = volume_ref[...].astype(F32)
    volume = [rows_ref[:, far * CHANNELS + c, :].astype(BF16) for c in range(CHANNELS) for far in range(2)]
    volume = jnp.concatenate(volume, axis=0)
    for j in range(BANK // 2):
        both = jnp.concatenate([basis_ref[2 * j], basis_ref[2 * j + 1]], axis=1)
        table = jnp.dot(volume, both, preferred_element_type=F32)
        high, low = split(table)
        for p in range(2):
            row = (2 * j + p) * HALF
            for c in range(CHANNELS):
                piece = (slice(c * HALF, (c + 1) * HALF), slice(p * DEPTH, (p + 1) * DEPTH))
                high_ref[row : row + HALF, c * DEPTH : (c + 1) * DEPTH] = high[piece]
                low_ref[row : row + HALF, c * DEPTH : (c + 1) * DEPTH] = low[piece]
    picks = picks_ref[core]
    return jnp.dot(picks, high_ref[...], preferred_element_type=F32) + jnp.dot(
        picks, low_ref[...], preferred_element_type=F32
    )


def back_project(core, rounded, basis_ref, places_ref, grad_ref, high_ref, low_ref):
    for j in range(BANK // 4):
        places = places_ref[core, j * 128 : (j + 1) * 128, :][:, :PAIRS]
        summed = jnp.dot(places, rounded, preferred_element_type=F32)
        high, low = split(summed)
        for p in range(4):
            col = (4 * j + p) * DEPTH
            for c in range(CHANNELS):
                piece = (slice(p * HALF, (p + 1) * HALF), slice(c * DEPTH, (c + 1) * DEPTH))
                high_ref[c * HALF : (c + 1) * HALF, col : col + DEPTH] = high[piece]
                low_ref[c * HALF : (c + 1) * HALF, col : col + DEPTH] = low[piece]
    bank = jnp.concatenate([basis_ref[p] for p in range(BANK)], axis=1)
    turned = (((1,), (1,)), ((), ()))
    total = lax.dot_general(high_ref[...], bank, turned, preferred_element_type=F32) + lax.dot_general(
        low_ref[...], bank, turned, preferred_element_type=F32
    )
    for c in range(CHANNELS):
        for far in range(2):
            row = c * HALF + far * SPOTS
            grad_ref[:, far * CHANNELS + c, :] = total[row : row + SPOTS]


def first_kernel(volume_ref, basis_ref, picks_ref, lines_ref, rows_ref, high_ref, low_ref):
    lines_ref[...] = project(0, volume_ref, basis_ref, picks_ref, rows_ref, high_ref, low_ref)


def second_kernel(
    volume_ref,
    basis_ref,
    picks_ref,
    places_ref,
    lines_ref,
    message0_ref,
    message1_ref,
    message2_ref,
    message3_ref,
    rounded_ref,
    grad_ref,
    rows_ref,
    high_ref,
    low_ref,
    zhigh_ref,
    zlow_ref,
):
    lines = lines_ref[...] + project(1, volume_ref, basis_ref, picks_ref, rows_ref, high_ref, low_ref)
    line = [lines[:, m * SPAN : (m + 1) * SPAN] for m in range(3)]
    grads = [jnp.zeros((PAIRS, SPAN), F32) for m in range(3)]
    for message_ref in (message0_ref, message1_ref, message2_ref, message3_ref):
        figures = message_ref[2 * PAIRS : 2 * PAIRS + 16, :].astype(F32)
        figures = (figures[:, :128] + figures[:, 128:256]) + figures[:, 256:384]
        figures = jnp.concatenate([figures] * QUARTERS, axis=1)
        for b in range(2):
            weight = [figures[4 * b + m : 4 * b + m + 1, :] for m in range(4)]
            exponent = weight[0] * line[0] + weight[1] * line[1] + weight[2] * line[2]
            photons = message_ref[b * PAIRS : (b + 1) * PAIRS, :].astype(F32)
            misfit = photons - weight[3] * jnp.exp(-exponent)
            grads = [grads[m] + weight[m] * misfit for m in range(3)]
    rounded = jnp.concatenate([g.astype(BF16) for g in grads], axis=1)
    rounded_ref[...] = rounded
    back_project(1, rounded, basis_ref, places_ref, grad_ref, zhigh_ref, zlow_ref)


def third_kernel(rounded_ref, basis_ref, places_ref, grad_ref, zhigh_ref, zlow_ref):
    back_project(0, rounded_ref[...], basis_ref, places_ref, grad_ref, zhigh_ref, zlow_ref)


def call(kernel, out_shape, forward, backward, *operands):
    vmem = pl.BlockSpec(memory_space=pltpu.VMEM)
    scratch = []
    if forward:
        scratch += [pltpu.VMEM((SPOTS, BLOCK, WIDTH), F32)]
        scratch += [pltpu.VMEM((BANK * HALF, CHANNELS * DEPTH), BF16)] * 2
    if backward:
        scratch += [pltpu.VMEM((CHANNELS * HALF, BANK * DEPTH), BF16)] * 2
    return pl.pallas_call(
        kernel,
        out_shape=out_shape,
        in_specs=[vmem] * len(operands),
        out_specs=[vmem] * len(out_shape),
        scratch_shapes=scratch,
        compiler_params=pltpu.CompilerParams(vmem_limit_bytes=40 * 2**20),
    )(*operands)


def on_device(volume, basis, tile_index, tile_offset, attenuation, flux, counts):
    view = lax.axis_index("view")
    far = (view >> 1) & 1
    quarter = lax.axis_index("bin") ^ (2 * far)
    views, det_tiles, band = tile_index.shape
    slices = volume.shape[2]
    own_slices = slices // QUARTERS
    plane_groups = groups_of(PLANE)
    line_groups = groups_of(255 ^ LINE)

    mine = lax.dynamic_slice_in_dim(volume[0], quarter * own_slices, own_slices, 1).reshape(CHANNELS, WIDTH)
    theirs = lax.ppermute(mine, BOTH, partners(FAR))
    stack = jnp.concatenate([mine, theirs], axis=0)

    figures = jnp.concatenate([attenuation, flux[:, None]], axis=1).reshape(8)
    first = lax.reduce_precision(figures, 8, 7)
    rest = figures - first
    second = lax.reduce_precision(rest, 8, 7)
    third = rest - second
    figures = jnp.stack([first, second, third, jnp.zeros_like(third)], axis=1).astype(BF16)
    figures = jnp.broadcast_to(figures[:, :, None], (8, QUARTERS, DEPTH)).reshape(8, SPAN)
    figures = jnp.pad(figures, ((0, 8), (0, 0)))
    photons = counts.astype(BF16).reshape(views, 2, QUARTERS, own_slices, det_tiles, DEPTH)
    photons = photons.transpose(2, 1, 0, 4, 3, 5).reshape(QUARTERS, 2 * PAIRS, SPAN)
    messages = jnp.concatenate([photons, jnp.broadcast_to(figures[None], (QUARTERS, 16, SPAN))], axis=1)
    payloads = [lax.dynamic_index_in_dim(messages, quarter ^ shift, 0, keepdims=False) for shift in range(QUARTERS)]
    stack, payloads = lax.optimization_barrier((stack, payloads))

    stack = jnp.broadcast_to(stack[None], (SPOTS, BLOCK, WIDTH))
    own = lax.all_to_all(stack, BOTH, 0, 0, tiled=True, axis_index_groups=plane_groups)
    arrived = payloads[:1] + [lax.ppermute(payloads[shift], BOTH, partners(shift)) for shift in range(1, QUARTERS)]

    index = tile_index.reshape(PAIRS, band) ^ (view & 3)
    index = (index & 1) * HALF + ((index >> 1) & 1) * SPOTS + (index >> 2)
    index = jnp.pad(index.T, ((0, 0), (0, 128 - PAIRS)))
    offset = jnp.pad(tile_offset.reshape(PAIRS, band).T, ((0, 0), (0, 128 - PAIRS)))
    picks, places = select(index, offset)

    other = lax.ppermute(own, BOTH, partners(CORE))
    lines_shape = jax.ShapeDtypeStruct((PAIRS, CHANNELS * DEPTH), F32)
    rounded_shape = jax.ShapeDtypeStruct((PAIRS, CHANNELS * DEPTH), BF16)
    grad_shape = jax.ShapeDtypeStruct((SPOTS, BLOCK, WIDTH), F32)
    (lines,) = call(first_kernel, [lines_shape], True, False, own, basis, picks)
    rounded, send = call(
        second_kernel, [rounded_shape, grad_shape], True, True, other, basis, picks, places, lines, *arrived
    )
    received = lax.ppermute(send, BOTH, partners(CORE))
    (keep,) = call(third_kernel, [grad_shape], False, True, rounded, basis, places)

    parts = lax.all_to_all(keep + received, BOTH, 0, 0, tiled=True, axis_index_groups=plane_groups)
    total = jnp.sum(parts, axis=0)
    scale = 1.0 / (8.0 * math.sqrt(views * lax.axis_size("view")))
    total = (total * scale).reshape(2, CHANNELS, WIDTH)
    blocks = jnp.where(far == 0, total, total[::-1])
    blocks = jnp.broadcast_to(blocks[:, None], (2, QUARTERS, CHANNELS, WIDTH)).reshape(2 * QUARTERS, CHANNELS, WIDTH)
    blocks = lax.all_to_all(blocks, BOTH, 0, 0, tiled=True, axis_index_groups=line_groups)
    quarters = blocks[:4] + jnp.concatenate([blocks[6:], blocks[4:6]], axis=0)
    quarters = quarters.reshape(QUARTERS, 3, own_slices, WIDTH).transpose(1, 0, 2, 3)
    return quarters.reshape(1, 3, slices, WIDTH)


def solution(mesh):
    placed = (
        P("view", None, None, None),
        P(),
        P("view", None, None),
        P("view", None, None),
        P("bin", None),
        P("bin"),
        P("view", "bin", None, None),
    )
    return jax.shard_map(
        on_device,
        mesh=mesh,
        in_specs=placed,
        out_specs=P("view", None, None, None),
        check_vma=False,
    )
```

```python
import math

import jax
import jax.numpy as jnp
from jax import lax
from jax.experimental import pallas as pl
from jax.experimental.pallas import tpu as pltpu
from jax.sharding import PartitionSpec as P

BOTH = ("view", "bin")
BF16 = jnp.bfloat16
F32 = jnp.float32

CORE = 4
FAR = 8 + 2
PLANE = 15
LINE = 11

SPOTS = 16
HALF = 32
TILES = 64
QUARTERS = 4
CHANNELS = 6
PAIRS = 48
BANK = 16
WIDTH = 256
DEPTH = 128
SPAN = 2 * DEPTH
BLOCK = 2 * CHANNELS


def partners(mask):
    return [(place, place ^ mask) for place in range(256)]


def groups_of(same):
    return [[place for place in range(256) if place & same == rest] for rest in range(256) if rest & same == rest]


def split(value):
    high = value.astype(BF16)
    low = (value - high.astype(F32)).astype(BF16)
    return high, low


def select(code_ref, square_ref):
    square_ref[...] = jnp.zeros((128, 128), F32)
    square_ref[: 2 * PAIRS, : code_ref.shape[1]] = code_ref[...].astype(F32)
    code = square_ref[...].T.astype(jnp.int32)
    labels = lax.broadcasted_iota(jnp.int32, (TILES, 128), 0)
    chosen = jnp.full((TILES, 128), -1, jnp.int32)
    for step in range(code_ref.shape[1]):
        row = code[step : step + 1, :]
        chosen = jnp.where(labels == (row & (TILES - 1)), row >> 6, chosen)
    return chosen.astype(F32)


def message_kernel(counts_ref, attenuation_ref, flux_ref, message0_ref, message1_ref, message2_ref, message3_ref, rows_ref):
    view = lax.axis_index("view")
    quarter = lax.axis_index("bin") ^ (2 * ((view >> 1) & 1))
    for v in range(4):
        for b in range(2):
            for s in range(0, 16, 8):
                piece = counts_ref[v, b, s : s + 8, :].astype(F32)
                piece = jnp.stack([piece[:, d * DEPTH : (d + 1) * DEPTH] for d in range(12)])
                row = b * PAIRS + v * 12
                rows_ref[s : s + 8, row : row + 12, :] = jnp.swapaxes(piece, 0, 1)
    refs = (message0_ref, message1_ref, message2_ref, message3_ref)
    for shift, ref in enumerate(refs):
        for s in range(4):
            piece = rows_ref[(quarter ^ shift) * 4 + s].astype(BF16)
            ref[: 2 * PAIRS, s * DEPTH : (s + 1) * DEPTH] = piece
    labels = lax.broadcasted_iota(jnp.int32, (8, DEPTH), 0)
    value = jnp.zeros((8, DEPTH), F32)
    for b in range(2):
        for m in range(4):
            figure = attenuation_ref[b, m] if m < 3 else flux_ref[b]
            value = jnp.where(labels == 4 * b + m, figure, value)
    first = value.astype(BF16)
    rest = value - first.astype(F32)
    second = rest.astype(BF16)
    third = (rest - second.astype(F32)).astype(BF16)
    upper = jnp.concatenate([first.astype(F32), second.astype(F32)], axis=1)
    lower = jnp.concatenate([third.astype(F32), jnp.zeros((8, DEPTH), F32)], axis=1)
    figures = jnp.concatenate([upper, lower], axis=0).astype(BF16)
    figures = jnp.concatenate([figures, figures], axis=1)
    for ref in refs:
        ref[2 * PAIRS :, :] = figures


def local_kernel(
    code_ref,
    volume_ref,
    basis_ref,
    mine_ref,
    theirs_ref,
    grad_ref,
    square_ref,
    rows_ref,
    high_ref,
    low_ref,
    zhigh_ref,
    zlow_ref,
):
    rows_ref[...] = volume_ref[...].astype(F32)
    volume = [rows_ref[:, near * CHANNELS + c, :].astype(BF16) for c in range(CHANNELS) for near in range(4)]
    volume = jnp.concatenate(volume, axis=0)
    for j in range(BANK // 2):
        both = jnp.concatenate([basis_ref[2 * j], basis_ref[2 * j + 1]], axis=1)
        table = jnp.dot(volume, both, preferred_element_type=F32)
        high, low = split(table)
        for p in range(2):
            row = (2 * j + p) * TILES
            for c in range(CHANNELS):
                piece = (slice(c * TILES, (c + 1) * TILES), slice(p * DEPTH, (p + 1) * DEPTH))
                high_ref[row : row + TILES, c * DEPTH : (c + 1) * DEPTH] = high[piece]
                low_ref[row : row + TILES, c * DEPTH : (c + 1) * DEPTH] = low[piece]
    chosen = select(code_ref, square_ref)
    part = (lax.broadcasted_iota(jnp.int32, (2 * PAIRS, 128), 1) // TILES).astype(F32)
    turned = jnp.concatenate([chosen, chosen], axis=0).T[: 2 * PAIRS] - part
    picks = jnp.concatenate([(turned == 2 * j).astype(F32).astype(BF16) for j in range(BANK // 2)], axis=1)
    lines = jnp.dot(picks, high_ref[...], preferred_element_type=F32) + jnp.dot(
        picks, low_ref[...], preferred_element_type=F32
    )

    line = [lines[:, m * SPAN : (m + 1) * SPAN] for m in range(3)]
    grads = [jnp.zeros((2 * PAIRS, SPAN), F32) for m in range(3)]
    for source in range(QUARTERS):
        figures = mine_ref[source, 2 * PAIRS :, :].astype(F32)
        figures = (figures[:8, :DEPTH] + figures[:8, DEPTH:]) + figures[8:, :DEPTH]
        figures = jnp.concatenate([figures] * 2, axis=1)
        for b in range(2):
            weight = [figures[4 * b + m : 4 * b + m + 1, :] for m in range(4)]
            exponent = weight[0] * line[0] + weight[1] * line[1] + weight[2] * line[2]
            photons = [ref[source, b * PAIRS : (b + 1) * PAIRS, :] for ref in (mine_ref, theirs_ref)]
            photons = jnp.concatenate(photons, axis=0).astype(F32)
            misfit = photons - weight[3] * jnp.exp(-exponent)
            grads = [grads[m] + weight[m] * misfit for m in range(3)]
    rounded = jnp.concatenate([g.astype(BF16) for g in grads], axis=1)

    chosen = chosen[:, : 2 * PAIRS]
    for j in range(BANK // 2):
        places = [(chosen == 2 * j + p).astype(F32).astype(BF16) for p in range(2)]
        summed = jnp.dot(jnp.concatenate(places, axis=0), rounded, preferred_element_type=F32)
        high, low = split(summed)
        for p in range(2):
            col = (2 * j + p) * DEPTH
            for c in range(CHANNELS):
                piece = (slice(p * TILES, (p + 1) * TILES), slice(c * DEPTH, (c + 1) * DEPTH))
                zhigh_ref[c * TILES : (c + 1) * TILES, col : col + DEPTH] = high[piece]
                zlow_ref[c * TILES : (c + 1) * TILES, col : col + DEPTH] = low[piece]
    bank = jnp.concatenate([basis_ref[p] for p in range(BANK)], axis=1)
    turn = (((1,), (1,)), ((), ()))
    total = lax.dot_general(zhigh_ref[...], bank, turn, preferred_element_type=F32) + lax.dot_general(
        zlow_ref[...], bank, turn, preferred_element_type=F32
    )
    for c in range(CHANNELS):
        for near in range(4):
            row = c * TILES + near * SPOTS
            grad_ref[:, near * CHANNELS + c, :] = total[row : row + SPOTS]


def local(*operands):
    vmem = pl.BlockSpec(memory_space=pltpu.VMEM)
    return pl.pallas_call(
        local_kernel,
        out_shape=jax.ShapeDtypeStruct((SPOTS, 2 * BLOCK, WIDTH), F32),
        in_specs=[vmem] * len(operands),
        out_specs=vmem,
        scratch_shapes=[
            pltpu.VMEM((128, 128), F32),
            pltpu.VMEM((SPOTS, 2 * BLOCK, WIDTH), F32),
            pltpu.VMEM((BANK * TILES, CHANNELS * DEPTH), BF16),
            pltpu.VMEM((BANK * TILES, CHANNELS * DEPTH), BF16),
            pltpu.VMEM((CHANNELS * TILES, BANK * DEPTH), BF16),
            pltpu.VMEM((CHANNELS * TILES, BANK * DEPTH), BF16),
        ],
        compiler_params=pltpu.CompilerParams(vmem_limit_bytes=32 * 2**20),
    )(*operands)


def on_device(volume, basis, tile_index, tile_offset, attenuation, flux, counts):
    view = lax.axis_index("view")
    core = view & 1
    far = (view >> 1) & 1
    quarter = lax.axis_index("bin") ^ (2 * far)
    views, det_tiles, band = tile_index.shape
    slices = volume.shape[2]
    plane_groups = groups_of(PLANE)
    line_groups = groups_of(255 ^ LINE)

    def eighth(of_core):
        return lax.dynamic_slice_in_dim(volume[0], quarter * 4 + of_core * 2, 2, 1).reshape(CHANNELS, WIDTH)

    mine = eighth(core)
    theirs = lax.ppermute(eighth(1 - core), BOTH, partners(CORE))
    near = jnp.where(core == 0, jnp.concatenate([mine, theirs]), jnp.concatenate([theirs, mine]))
    stack = jnp.concatenate([near, lax.ppermute(near, BOTH, partners(FAR))], axis=0)

    vmem = pl.BlockSpec(memory_space=pltpu.VMEM)
    smem = pl.BlockSpec(memory_space=pltpu.SMEM)
    messages = pl.pallas_call(
        message_kernel,
        out_shape=[jax.ShapeDtypeStruct((2 * PAIRS + 16, 2 * SPAN), BF16)] * QUARTERS,
        in_specs=[vmem, smem, smem],
        out_specs=[vmem] * QUARTERS,
        scratch_shapes=[pltpu.VMEM((16, 2 * PAIRS, DEPTH), F32)],
    )(counts, attenuation, flux)

    stack, messages = lax.optimization_barrier((stack, messages))
    stack = jnp.broadcast_to(stack[None], (SPOTS, 2 * BLOCK, WIDTH))
    tiles = lax.all_to_all(stack, BOTH, 0, 0, tiled=True, axis_index_groups=plane_groups)

    code = tile_index.reshape(PAIRS, band) + TILES * tile_offset.reshape(PAIRS, band)
    code = jnp.concatenate([code, lax.ppermute(code, BOTH, partners(CORE))], axis=0)
    index = code & (TILES - 1)
    index = (((index >> 1) & 1) ^ far) * 2 * SPOTS + (index & 1) * SPOTS + (index >> 2)
    code = index | (code & -TILES)

    arrived = [lax.ppermute(messages[shift], BOTH, partners(shift)) if shift else messages[0] for shift in range(QUARTERS)]
    arrived = jnp.stack(arrived)
    keep = lax.dynamic_slice_in_dim(arrived, core * SPAN, SPAN, 2)
    other = lax.dynamic_slice_in_dim(arrived[:, : 2 * PAIRS], (1 - core) * SPAN, SPAN, 2)
    other = lax.ppermute(other, BOTH, partners(CORE))

    grads = local(code, tiles, basis, keep, other)

    nearer, first = far == 0, core == 0
    grads, nearer, first = lax.optimization_barrier((grads, nearer, first))
    parts = lax.all_to_all(grads, BOTH, 0, 0, tiled=True, axis_index_groups=plane_groups)
    total = jnp.sum(parts, axis=0)
    scale = 1.0 / (8.0 * math.sqrt(views * lax.axis_size("view")))
    total = (total * scale).reshape(2, 2, CHANNELS, WIDTH)
    mine = jnp.where(first, total[:, 0], total[:, 1])
    theirs = lax.ppermute(jnp.where(first, total[:, 1], total[:, 0]), BOTH, partners(CORE))
    total = jnp.where(first, jnp.stack([mine, theirs], axis=1), jnp.stack([theirs, mine], axis=1))
    total = jnp.where(nearer, total, total[::-1]).reshape(2, 1, BLOCK, WIDTH)
    blocks = jnp.broadcast_to(total, (2, QUARTERS, BLOCK, WIDTH)).reshape(2 * QUARTERS, BLOCK, WIDTH)
    blocks = lax.all_to_all(blocks, BOTH, 0, 0, tiled=True, axis_index_groups=line_groups)
    quarters = blocks[:4] + jnp.concatenate([blocks[6:], blocks[4:6]], axis=0)
    quarters = quarters.reshape(QUARTERS, 2, 3, 2, WIDTH).transpose(2, 0, 1, 3, 4)
    return quarters.reshape(1, 3, slices, WIDTH)


def solution(mesh):
    placed = (
        P("view", None, None, None),
        P(),
        P("view", None, None),
        P("view", None, None),
        P("bin", None),
        P("bin"),
        P("view", "bin", None, None),
    )
    return jax.shard_map(
        on_device,
        mesh=mesh,
        in_specs=placed,
        out_specs=P("view", None, None, None),
        check_vma=False,
    )
```

```python
import math

import jax
import jax.numpy as jnp
from jax import lax
from jax.experimental import pallas as pl
from jax.experimental.pallas import tpu as pltpu
from jax.sharding import PartitionSpec as P

BOTH = ("view", "bin")
BF16 = jnp.bfloat16
F32 = jnp.float32

CORE = 4
FAR = 8 + 2
PLANE = 15
LINE = 11

SPOTS = 16
HALF = 32
HALF = 32
TILES = 64
QUARTERS = 4
CHANNELS = 6
PAIRS = 48
BANK = 16
WIDTH = 256
DEPTH = 128
SPAN = 2 * DEPTH
BLOCK = 2 * CHANNELS


def partners(mask):
    return [(place, place ^ mask) for place in range(256)]


def groups_of(same):
    return [[place for place in range(256) if place & same == rest] for rest in range(256) if rest & same == rest]


def split(value):
    high = value.astype(BF16)
    low = (value - high.astype(F32)).astype(BF16)
    return high, low


def select(code_ref, square_ref):
    square_ref[...] = jnp.zeros((128, 128), F32)
    square_ref[: 2 * PAIRS, : code_ref.shape[1]] = code_ref[...].astype(F32)
    code = square_ref[...].T.astype(jnp.int32)
    labels = lax.broadcasted_iota(jnp.int32, (TILES, 128), 0)
    chosen = jnp.full((TILES, 128), -1, jnp.int32)
    for step in range(code_ref.shape[1]):
        row = code[step : step + 1, :]
        chosen = jnp.where(labels == (row & (TILES - 1)), row >> 6, chosen)
    return chosen.astype(F32)


def message_kernel(counts_ref, attenuation_ref, flux_ref, message0_ref, message1_ref, message2_ref, message3_ref, rows_ref):
    view = lax.axis_index("view")
    quarter = lax.axis_index("bin") ^ (2 * ((view >> 1) & 1))
    for v in range(4):
        for b in range(2):
            for s in range(0, 16, 8):
                piece = counts_ref[v, b, s : s + 8, :].astype(F32)
                piece = jnp.stack([piece[:, d * DEPTH : (d + 1) * DEPTH] for d in range(12)])
                row = b * PAIRS + v * 12
                rows_ref[s : s + 8, row : row + 12, :] = jnp.swapaxes(piece, 0, 1)
    refs = (message0_ref, message1_ref, message2_ref, message3_ref)
    for shift, ref in enumerate(refs):
        for s in range(4):
            piece = rows_ref[(quarter ^ shift) * 4 + s].astype(BF16)
            ref[: 2 * PAIRS, s * DEPTH : (s + 1) * DEPTH] = piece
    labels = lax.broadcasted_iota(jnp.int32, (8, DEPTH), 0)
    value = jnp.zeros((8, DEPTH), F32)
    for b in range(2):
        for m in range(4):
            figure = attenuation_ref[b, m] if m < 3 else flux_ref[b]
            value = jnp.where(labels == 4 * b + m, figure, value)
    first = value.astype(BF16)
    rest = value - first.astype(F32)
    second = rest.astype(BF16)
    third = (rest - second.astype(F32)).astype(BF16)
    upper = jnp.concatenate([first.astype(F32), second.astype(F32)], axis=1)
    lower = jnp.concatenate([third.astype(F32), jnp.zeros((8, DEPTH), F32)], axis=1)
    figures = jnp.concatenate([upper, lower], axis=0).astype(BF16)
    figures = jnp.concatenate([figures, figures], axis=1)
    for ref in refs:
        ref[2 * PAIRS :, :] = figures


def halves_kernel(mine_ref, theirs_ref, keep_ref, send_ref):
    first = lax.axis_index("view") & 1 == 0
    for far, ref in enumerate((mine_ref, theirs_ref)):
        rows = ref[...].astype(F32)
        parts = [jnp.concatenate([rows[m * 4 + 2 * c : m * 4 + 2 * c + 2] for m in range(3)], axis=0) for c in range(2)]
        keep_ref[far] = jnp.where(first, *parts).astype(BF16)
        send_ref[far] = jnp.where(first, *parts[::-1]).astype(BF16)


def forward_kernel(code_ref, volume_ref, basis_ref, chosen_ref, lines_ref, square_ref, rows_ref, high_ref, low_ref):
    rows_ref[...] = volume_ref[...].astype(F32)
    volume = [rows_ref[:, near * CHANNELS + c, :].astype(BF16) for c in range(CHANNELS) for near in range(4)]
    volume = jnp.concatenate(volume, axis=0)
    for j in range(BANK // 2):
        both = jnp.concatenate([basis_ref[2 * j], basis_ref[2 * j + 1]], axis=1)
        table = jnp.dot(volume, both, preferred_element_type=F32)
        high, low = split(table)
        for p in range(2):
            row = (2 * j + p) * TILES
            for c in range(CHANNELS):
                piece = (slice(c * TILES, (c + 1) * TILES), slice(p * DEPTH, (p + 1) * DEPTH))
                high_ref[row : row + TILES, c * DEPTH : (c + 1) * DEPTH] = high[piece]
                low_ref[row : row + TILES, c * DEPTH : (c + 1) * DEPTH] = low[piece]
    chosen = select(code_ref, square_ref)
    chosen_ref[...] = chosen
    part = (lax.broadcasted_iota(jnp.int32, (2 * PAIRS, 128), 1) // TILES).astype(F32)
    turned = jnp.concatenate([chosen, chosen], axis=0).T[: 2 * PAIRS] - part
    picks = jnp.concatenate([(turned == 2 * j).astype(F32).astype(BF16) for j in range(BANK // 2)], axis=1)
    lines_ref[...] = jnp.dot(picks, high_ref[...], preferred_element_type=F32) + jnp.dot(
        picks, low_ref[...], preferred_element_type=F32
    )


def residual_kernel(lines_ref, mine_ref, theirs_ref, rounded_ref):
    line = [lines_ref[:, m * SPAN : (m + 1) * SPAN] for m in range(3)]
    grads = [jnp.zeros((2 * PAIRS, SPAN), F32) for m in range(3)]
    for source in range(QUARTERS):
        figures = mine_ref[source, 2 * PAIRS :, :].astype(F32)
        figures = (figures[:8, :DEPTH] + figures[:8, DEPTH:]) + figures[8:, :DEPTH]
        figures = jnp.concatenate([figures] * 2, axis=1)
        for b in range(2):
            weight = [figures[4 * b + m : 4 * b + m + 1, :] for m in range(4)]
            exponent = weight[0] * line[0] + weight[1] * line[1] + weight[2] * line[2]
            photons = [ref[source, b * PAIRS : (b + 1) * PAIRS, :] for ref in (mine_ref, theirs_ref)]
            photons = jnp.concatenate(photons, axis=0).astype(F32)
            misfit = photons - weight[3] * jnp.exp(-exponent)
            grads = [grads[m] + weight[m] * misfit for m in range(3)]
    for m in range(3):
        rounded_ref[:, m * SPAN : (m + 1) * SPAN] = grads[m].astype(BF16)


def back_project(rounded, chosen_ref, basis_ref, high_ref, low_ref):
    own = [chosen_ref[far * 2 * SPOTS : far * 2 * SPOTS + SPOTS, : 2 * PAIRS] for far in range(2)]
    own = jnp.concatenate(own, axis=0)
    for j in range(BANK // 4):
        places = [(own == 4 * j + p).astype(F32).astype(BF16) for p in range(4)]
        summed = jnp.dot(jnp.concatenate(places, axis=0), rounded, preferred_element_type=F32)
        high, low = split(summed)
        for p in range(4):
            col = (4 * j + p) * DEPTH
            for c in range(CHANNELS):
                piece = (slice(p * HALF, (p + 1) * HALF), slice(c * DEPTH, (c + 1) * DEPTH))
                high_ref[c * HALF : (c + 1) * HALF, col : col + DEPTH] = high[piece]
                low_ref[c * HALF : (c + 1) * HALF, col : col + DEPTH] = low[piece]
    bank = jnp.concatenate([basis_ref[p] for p in range(BANK)], axis=1)
    turn = (((1,), (1,)), ((), ()))
    return lax.dot_general(high_ref[...], bank, turn, preferred_element_type=F32) + lax.dot_general(
        low_ref[...], bank, turn, preferred_element_type=F32
    )


def own_kernel(rounded_ref, chosen_ref, basis_ref, total_ref, high_ref, low_ref):
    total_ref[...] = back_project(rounded_ref[...], chosen_ref, basis_ref, high_ref, low_ref)


def other_kernel(rounded_ref, chosen_ref, basis_ref, total_ref, grad_ref, high_ref, low_ref):
    rounded = jnp.concatenate([rounded_ref[PAIRS:], rounded_ref[:PAIRS]], axis=0)
    other = back_project(rounded, chosen_ref, basis_ref, high_ref, low_ref)
    own = total_ref[...]
    view = lax.axis_index("view")
    halves = jnp.where(view & 1 == 0, own, other), jnp.where(view & 1 == 0, other, own)
    for core in range(2):
        for c in range(CHANNELS):
            pair = halves[core][c * HALF : (c + 1) * HALF]
            first, second = pair[:SPOTS], pair[SPOTS:]
            grad_ref[:, core * CHANNELS + c, :] = jnp.where(view & 2 == 0, first, second)
            grad_ref[:, BLOCK + core * CHANNELS + c, :] = jnp.where(view & 2 == 0, second, first)


FORWARD = [
    pltpu.VMEM((128, 128), F32),
    pltpu.VMEM((SPOTS, 2 * BLOCK, WIDTH), F32),
    pltpu.VMEM((BANK * TILES, CHANNELS * DEPTH), BF16),
    pltpu.VMEM((BANK * TILES, CHANNELS * DEPTH), BF16),
]
BACKWARD = [pltpu.VMEM((CHANNELS * HALF, BANK * DEPTH), BF16)] * 2


def call(kernel, out_shape, scratch, *operands):
    vmem = pl.BlockSpec(memory_space=pltpu.VMEM)
    return pl.pallas_call(
        kernel,
        out_shape=out_shape,
        in_specs=[vmem] * len(operands),
        out_specs=jax.tree.map(lambda _: vmem, out_shape),
        scratch_shapes=scratch,
        compiler_params=pltpu.CompilerParams(vmem_limit_bytes=32 * 2**20),
    )(*operands)


def on_device(volume, basis, tile_index, tile_offset, attenuation, flux, counts):
    view = lax.axis_index("view")
    core = view & 1
    far = (view >> 1) & 1
    quarter = lax.axis_index("bin") ^ (2 * far)
    views, det_tiles, band = tile_index.shape
    slices = volume.shape[2]
    plane_groups = groups_of(PLANE)
    line_groups = groups_of(255 ^ LINE)

    mine = lax.dynamic_slice_in_dim(volume[0], quarter * 4, 4, 1).reshape(2 * CHANNELS, WIDTH)
    theirs = lax.ppermute(mine, BOTH, partners(FAR))

    vmem = pl.BlockSpec(memory_space=pltpu.VMEM)
    smem = pl.BlockSpec(memory_space=pltpu.SMEM)
    messages = pl.pallas_call(
        message_kernel,
        out_shape=[jax.ShapeDtypeStruct((2 * PAIRS + 16, 2 * SPAN), BF16)] * QUARTERS,
        in_specs=[vmem, smem, smem],
        out_specs=[vmem] * QUARTERS,
        scratch_shapes=[pltpu.VMEM((16, 2 * PAIRS, DEPTH), F32)],
        compiler_params=pltpu.CompilerParams(vmem_limit_bytes=8 * 2**20),
    )(counts, attenuation, flux)

    mine, theirs = pl.pallas_call(
        halves_kernel,
        out_shape=[jax.ShapeDtypeStruct((2, CHANNELS, WIDTH), BF16)] * 2,
        in_specs=[vmem] * 2,
        out_specs=[vmem] * 2,
        compiler_params=pltpu.CompilerParams(vmem_limit_bytes=4 * 2**20),
        cost_estimate=pl.CostEstimate(flops=0, bytes_accessed=10**8, transcendentals=0),
    )(mine, theirs)
    theirs = lax.ppermute(theirs, BOTH, partners(CORE))
    stack = jnp.stack([mine, theirs], axis=1)
    stack = jnp.broadcast_to(stack.reshape(1, 2 * BLOCK, WIDTH), (SPOTS, 2 * BLOCK, WIDTH))
    tiles = lax.all_to_all(stack, BOTH, 0, 0, tiled=True, axis_index_groups=plane_groups)

    arrived = [lax.ppermute(messages[shift], BOTH, partners(shift)) if shift else messages[0] for shift in range(QUARTERS)]
    arrived = jnp.stack(arrived)
    keep = lax.dynamic_slice_in_dim(arrived, core * SPAN, SPAN, 2)
    other = lax.dynamic_slice_in_dim(arrived[:, : 2 * PAIRS], (1 - core) * SPAN, SPAN, 2)

    code = tile_index.reshape(PAIRS, band) + TILES * tile_offset.reshape(PAIRS, band)
    other = lax.ppermute(other, BOTH, partners(CORE))
    code = jnp.concatenate([code, lax.ppermute(code, BOTH, partners(CORE))], axis=0)
    index = (code & (TILES - 1)) ^ (view & 3)
    index = ((index >> 1) & 1) * 2 * SPOTS + (index & 1) * SPOTS + (index >> 2)
    code = index | (code & -TILES)

    wide = CHANNELS * DEPTH
    chosen, lines = call(
        forward_kernel,
        [jax.ShapeDtypeStruct((TILES, 128), F32), jax.ShapeDtypeStruct((2 * PAIRS, wide), F32)],
        FORWARD,
        code,
        tiles,
        basis,
    )
    rounded = call(residual_kernel, jax.ShapeDtypeStruct((2 * PAIRS, wide), BF16), [], lines, keep, other)
    swapped = lax.ppermute(rounded, BOTH, partners(CORE))
    total = call(
        own_kernel, jax.ShapeDtypeStruct((CHANNELS * HALF, WIDTH), F32), BACKWARD, rounded, chosen, basis
    )
    grads = call(
        other_kernel,
        jax.ShapeDtypeStruct((SPOTS, 2 * BLOCK, WIDTH), F32),
        BACKWARD,
        swapped,
        chosen,
        basis,
        total,
    )

    parts = lax.all_to_all(grads, BOTH, 0, 0, tiled=True, axis_index_groups=plane_groups)
    scale = 1.0 / (8.0 * math.sqrt(views * lax.axis_size("view")))
    total = (jnp.sum(parts, axis=0) * scale).reshape(2, 1, BLOCK, WIDTH)
    blocks = jnp.broadcast_to(total, (2, QUARTERS, BLOCK, WIDTH)).reshape(2 * QUARTERS, BLOCK, WIDTH)
    blocks = lax.all_to_all(blocks, BOTH, 0, 0, tiled=True, axis_index_groups=line_groups)
    quarters = blocks[:4] + jnp.concatenate([blocks[6:], blocks[4:6]], axis=0)
    quarters = quarters.reshape(QUARTERS, 2, 3, 2, WIDTH).transpose(2, 0, 1, 3, 4)
    return quarters.reshape(1, 3, slices, WIDTH)


def solution(mesh):
    placed = (
        P("view", None, None, None),
        P(),
        P("view", None, None),
        P("view", None, None),
        P("bin", None),
        P("bin"),
        P("view", "bin", None, None),
    )
    return jax.shard_map(
        on_device,
        mesh=mesh,
        in_specs=placed,
        out_specs=P("view", None, None, None),
        check_vma=False,
    )
```

```python
import math

import jax
import jax.numpy as jnp
from jax import lax
from jax.experimental import pallas as pl
from jax.experimental.pallas import tpu as pltpu
from jax.sharding import PartitionSpec as P

BOTH = ("view", "bin")
BF16 = jnp.bfloat16
F32 = jnp.float32

CORE = 4
FAR = 8 + 2
PLANE = 15
LINE = 11

SPOTS = 16
HALF = 32
HALF = 32
TILES = 64
QUARTERS = 4
CHANNELS = 6
PAIRS = 48
BANK = 16
WIDTH = 256
DEPTH = 128
SPAN = 2 * DEPTH
BLOCK = 2 * CHANNELS


def partners(mask):
    return [(place, place ^ mask) for place in range(256)]


def groups_of(same):
    return [[place for place in range(256) if place & same == rest] for rest in range(256) if rest & same == rest]


def split(value):
    high = value.astype(BF16)
    low = (value - high.astype(F32)).astype(BF16)
    return high, low


def select(code_ref, square_ref):
    square_ref[...] = jnp.zeros((128, 128), F32)
    square_ref[: 2 * PAIRS, : code_ref.shape[1]] = code_ref[...].astype(F32)
    code = square_ref[...].T.astype(jnp.int32)
    labels = lax.broadcasted_iota(jnp.int32, (TILES, 128), 0)
    chosen = jnp.full((TILES, 128), -1, jnp.int32)
    for step in range(code_ref.shape[1]):
        row = code[step : step + 1, :]
        chosen = jnp.where(labels == (row & (TILES - 1)), row >> 6, chosen)
    return chosen.astype(F32)


def message_kernel(counts_ref, attenuation_ref, flux_ref, message0_ref, message1_ref, message2_ref, message3_ref, rows_ref):
    view = lax.axis_index("view")
    quarter = lax.axis_index("bin") ^ (2 * ((view >> 1) & 1))
    for v in range(4):
        for b in range(2):
            for s in range(0, 16, 8):
                piece = counts_ref[v, b, s : s + 8, :].astype(F32)
                piece = jnp.stack([piece[:, d * DEPTH : (d + 1) * DEPTH] for d in range(12)])
                row = b * PAIRS + v * 12
                rows_ref[s : s + 8, row : row + 12, :] = jnp.swapaxes(piece, 0, 1)
    refs = (message0_ref, message1_ref, message2_ref, message3_ref)
    for shift, ref in enumerate(refs):
        for s in range(4):
            piece = rows_ref[(quarter ^ shift) * 4 + s].astype(BF16)
            ref[: 2 * PAIRS, s * DEPTH : (s + 1) * DEPTH] = piece
    labels = lax.broadcasted_iota(jnp.int32, (8, DEPTH), 0)
    value = jnp.zeros((8, DEPTH), F32)
    for b in range(2):
        for m in range(4):
            figure = attenuation_ref[b, m] if m < 3 else flux_ref[b]
            value = jnp.where(labels == 4 * b + m, figure, value)
    first = value.astype(BF16)
    rest = value - first.astype(F32)
    second = rest.astype(BF16)
    third = (rest - second.astype(F32)).astype(BF16)
    upper = jnp.concatenate([first.astype(F32), second.astype(F32)], axis=1)
    lower = jnp.concatenate([third.astype(F32), jnp.zeros((8, DEPTH), F32)], axis=1)
    figures = jnp.concatenate([upper, lower], axis=0).astype(BF16)
    figures = jnp.concatenate([figures, figures], axis=1)
    for ref in refs:
        ref[2 * PAIRS :, :] = figures


def halves_kernel(mine_ref, theirs_ref, keep_ref, send_ref):
    first = lax.axis_index("view") & 1 == 0
    for far, ref in enumerate((mine_ref, theirs_ref)):
        rows = ref[...].astype(F32)
        parts = [jnp.concatenate([rows[m * 4 + 2 * c : m * 4 + 2 * c + 2] for m in range(3)], axis=0) for c in range(2)]
        keep_ref[far] = jnp.where(first, *parts).astype(BF16)
        send_ref[far] = jnp.where(first, *parts[::-1]).astype(BF16)


def forward_kernel(code_ref, volume_ref, basis_ref, chosen_ref, lines_ref, square_ref, rows_ref, parts_ref):
    rows_ref[...] = volume_ref[...].astype(F32)
    volume = [rows_ref[:, near * CHANNELS + c, :].astype(BF16) for c in range(CHANNELS) for near in range(4)]
    volume = jnp.concatenate(volume, axis=0)
    for j in range(BANK // 2):
        both = jnp.concatenate([basis_ref[2 * j], basis_ref[2 * j + 1]], axis=1)
        table = jnp.dot(volume, both, preferred_element_type=F32)
        for part, value in enumerate(split(table)):
            for p in range(2):
                row = (part * BANK + 2 * j + p) * TILES
                for c in range(CHANNELS):
                    piece = value[c * TILES : (c + 1) * TILES, p * DEPTH : (p + 1) * DEPTH]
                    parts_ref[row : row + TILES, c * DEPTH : (c + 1) * DEPTH] = piece
    chosen = select(code_ref, square_ref)
    chosen_ref[...] = chosen
    part = (lax.broadcasted_iota(jnp.int32, (2 * PAIRS, 128), 1) // TILES).astype(F32)
    turned = jnp.concatenate([chosen, chosen], axis=0).T[: 2 * PAIRS] - part
    picks = [(turned == 2 * j).astype(F32).astype(BF16) for j in range(BANK // 2)]
    lines_ref[...] = jnp.dot(jnp.concatenate(picks * 2, axis=1), parts_ref[...], preferred_element_type=F32)


def residual_kernel(lines_ref, mine_ref, theirs_ref, rounded_ref):
    line = [lines_ref[:, m * SPAN : (m + 1) * SPAN] for m in range(3)]
    grads = [jnp.zeros((2 * PAIRS, SPAN), F32) for m in range(3)]
    for source in range(QUARTERS):
        figures = mine_ref[source, 2 * PAIRS :, :].astype(F32)
        figures = (figures[:8, :DEPTH] + figures[:8, DEPTH:]) + figures[8:, :DEPTH]
        figures = jnp.concatenate([figures] * 2, axis=1)
        for b in range(2):
            weight = [figures[4 * b + m : 4 * b + m + 1, :] for m in range(4)]
            exponent = weight[0] * line[0] + weight[1] * line[1] + weight[2] * line[2]
            photons = [ref[source, b * PAIRS : (b + 1) * PAIRS, :] for ref in (mine_ref, theirs_ref)]
            photons = jnp.concatenate(photons, axis=0).astype(F32)
            misfit = photons - weight[3] * jnp.exp(-exponent)
            grads = [grads[m] + weight[m] * misfit for m in range(3)]
    for m in range(3):
        rounded_ref[:, m * SPAN : (m + 1) * SPAN] = grads[m].astype(BF16)


def back_project(rounded, chosen_ref, basis_ref, parts_ref):
    own = [chosen_ref[far * 2 * SPOTS : far * 2 * SPOTS + SPOTS, : 2 * PAIRS] for far in range(2)]
    own = jnp.concatenate(own, axis=0)
    for j in range(BANK // 4):
        places = [(own == 4 * j + p).astype(F32).astype(BF16) for p in range(4)]
        summed = jnp.dot(jnp.concatenate(places, axis=0), rounded, preferred_element_type=F32)
        for part, value in enumerate(split(summed)):
            for p in range(4):
                col = (4 * j + p) * DEPTH
                for c in range(CHANNELS):
                    row = (part * CHANNELS + c) * HALF
                    piece = value[p * HALF : (p + 1) * HALF, c * DEPTH : (c + 1) * DEPTH]
                    parts_ref[row : row + HALF, col : col + DEPTH] = piece
    bank = jnp.concatenate([basis_ref[p] for p in range(BANK)], axis=1)
    turn = (((1,), (1,)), ((), ()))
    total = lax.dot_general(parts_ref[...], bank, turn, preferred_element_type=F32)
    return total[: CHANNELS * HALF] + total[CHANNELS * HALF :]


def own_kernel(rounded_ref, chosen_ref, basis_ref, total_ref, parts_ref):
    total_ref[...] = back_project(rounded_ref[...], chosen_ref, basis_ref, parts_ref)


def other_kernel(rounded_ref, chosen_ref, basis_ref, total_ref, grad_ref, parts_ref):
    rounded = jnp.concatenate([rounded_ref[PAIRS:], rounded_ref[:PAIRS]], axis=0)
    other = back_project(rounded, chosen_ref, basis_ref, parts_ref)
    own = total_ref[...]
    view = lax.axis_index("view")
    halves = jnp.where(view & 1 == 0, own, other), jnp.where(view & 1 == 0, other, own)
    for core in range(2):
        for c in range(CHANNELS):
            pair = halves[core][c * HALF : (c + 1) * HALF]
            first, second = pair[:SPOTS], pair[SPOTS:]
            grad_ref[:, core * CHANNELS + c, :] = jnp.where(view & 2 == 0, first, second)
            grad_ref[:, BLOCK + core * CHANNELS + c, :] = jnp.where(view & 2 == 0, second, first)


FORWARD = [
    pltpu.VMEM((128, 128), F32),
    pltpu.VMEM((SPOTS, 2 * BLOCK, WIDTH), F32),
    pltpu.VMEM((2 * BANK * TILES, CHANNELS * DEPTH), BF16),
]
BACKWARD = [pltpu.VMEM((2 * CHANNELS * HALF, BANK * DEPTH), BF16)]


def call(kernel, out_shape, scratch, *operands):
    vmem = pl.BlockSpec(memory_space=pltpu.VMEM)
    return pl.pallas_call(
        kernel,
        out_shape=out_shape,
        in_specs=[vmem] * len(operands),
        out_specs=jax.tree.map(lambda _: vmem, out_shape),
        scratch_shapes=scratch,
        compiler_params=pltpu.CompilerParams(vmem_limit_bytes=32 * 2**20),
    )(*operands)


def on_device(volume, basis, tile_index, tile_offset, attenuation, flux, counts):
    view = lax.axis_index("view")
    core = view & 1
    far = (view >> 1) & 1
    quarter = lax.axis_index("bin") ^ (2 * far)
    views, det_tiles, band = tile_index.shape
    slices = volume.shape[2]
    plane_groups = groups_of(PLANE)
    line_groups = groups_of(255 ^ LINE)

    mine = lax.dynamic_slice_in_dim(volume[0], quarter * 4, 4, 1).reshape(2 * CHANNELS, WIDTH)
    theirs = lax.ppermute(mine, BOTH, partners(FAR))

    vmem = pl.BlockSpec(memory_space=pltpu.VMEM)
    smem = pl.BlockSpec(memory_space=pltpu.SMEM)
    messages = pl.pallas_call(
        message_kernel,
        out_shape=[jax.ShapeDtypeStruct((2 * PAIRS + 16, 2 * SPAN), BF16)] * QUARTERS,
        in_specs=[vmem, smem, smem],
        out_specs=[vmem] * QUARTERS,
        scratch_shapes=[pltpu.VMEM((16, 2 * PAIRS, DEPTH), F32)],
        compiler_params=pltpu.CompilerParams(vmem_limit_bytes=8 * 2**20),
    )(counts, attenuation, flux)

    mine, theirs = pl.pallas_call(
        halves_kernel,
        out_shape=[jax.ShapeDtypeStruct((2, CHANNELS, WIDTH), BF16)] * 2,
        in_specs=[vmem] * 2,
        out_specs=[vmem] * 2,
        compiler_params=pltpu.CompilerParams(vmem_limit_bytes=4 * 2**20),
        cost_estimate=pl.CostEstimate(flops=0, bytes_accessed=10**8, transcendentals=0),
    )(mine, theirs)
    theirs = lax.ppermute(theirs, BOTH, partners(CORE))
    stack = jnp.stack([mine, theirs], axis=1)
    stack = jnp.broadcast_to(stack.reshape(1, 2 * BLOCK, WIDTH), (SPOTS, 2 * BLOCK, WIDTH))
    tiles = lax.all_to_all(stack, BOTH, 0, 0, tiled=True, axis_index_groups=plane_groups)

    arrived = [lax.ppermute(messages[shift], BOTH, partners(shift)) if shift else messages[0] for shift in range(QUARTERS)]
    arrived = jnp.stack(arrived)
    keep = lax.dynamic_slice_in_dim(arrived, core * SPAN, SPAN, 2)
    other = lax.dynamic_slice_in_dim(arrived[:, : 2 * PAIRS], (1 - core) * SPAN, SPAN, 2)

    code = tile_index.reshape(PAIRS, band) + TILES * tile_offset.reshape(PAIRS, band)
    other, code = lax.optimization_barrier((other, code))
    other = lax.ppermute(other, BOTH, partners(CORE))
    code = jnp.concatenate([code, lax.ppermute(code, BOTH, partners(CORE))], axis=0)
    index = (code & (TILES - 1)) ^ (view & 3)
    index = ((index >> 1) & 1) * 2 * SPOTS + (index & 1) * SPOTS + (index >> 2)
    code = index | (code & -TILES)

    wide = CHANNELS * DEPTH
    chosen, lines = call(
        forward_kernel,
        [jax.ShapeDtypeStruct((TILES, 128), F32), jax.ShapeDtypeStruct((2 * PAIRS, wide), F32)],
        FORWARD,
        code,
        tiles,
        basis,
    )
    rounded = call(residual_kernel, jax.ShapeDtypeStruct((2 * PAIRS, wide), BF16), [], lines, keep, other)
    swapped = lax.ppermute(rounded, BOTH, partners(CORE))
    total = call(
        own_kernel, jax.ShapeDtypeStruct((CHANNELS * HALF, WIDTH), F32), BACKWARD, rounded, chosen, basis
    )
    grads = call(
        other_kernel,
        jax.ShapeDtypeStruct((SPOTS, 2 * BLOCK, WIDTH), F32),
        BACKWARD,
        swapped,
        chosen,
        basis,
        total,
    )

    parts = lax.all_to_all(grads, BOTH, 0, 0, tiled=True, axis_index_groups=plane_groups)
    scale = 1.0 / (8.0 * math.sqrt(views * lax.axis_size("view")))
    total = (jnp.sum(parts, axis=0) * scale).reshape(2, 1, BLOCK, WIDTH)
    blocks = jnp.broadcast_to(total, (2, QUARTERS, BLOCK, WIDTH)).reshape(2 * QUARTERS, BLOCK, WIDTH)
    blocks = lax.all_to_all(blocks, BOTH, 0, 0, tiled=True, axis_index_groups=line_groups)
    quarters = blocks[:4] + jnp.concatenate([blocks[6:], blocks[4:6]], axis=0)
    quarters = quarters.reshape(QUARTERS, 2, 3, 2, WIDTH).transpose(2, 0, 1, 3, 4)
    return quarters.reshape(1, 3, slices, WIDTH)


def solution(mesh):
    placed = (
        P("view", None, None, None),
        P(),
        P("view", None, None),
        P("view", None, None),
        P("bin", None),
        P("bin"),
        P("view", "bin", None, None),
    )
    return jax.shard_map(
        on_device,
        mesh=mesh,
        in_specs=placed,
        out_specs=P("view", None, None, None),
        check_vma=False,
    )
```

```python
import functools
import math

import jax
import jax.numpy as jnp
from jax import lax
from jax.experimental import pallas as pl
from jax.experimental.pallas import tpu as pltpu
from jax.sharding import PartitionSpec as P

BOTH = ("view", "bin")
BF16 = jnp.bfloat16
F32 = jnp.float32

CORE = 4
FAR = 8 + 2
PLANE = 15
LINE = 11

SPOTS = 16
HALF = 32
HALF = 32
TILES = 64
QUARTERS = 4
CHANNELS = 6
PAIRS = 48
BANK = 16
WIDTH = 256
DEPTH = 128
SPAN = 2 * DEPTH
BLOCK = 2 * CHANNELS
ROWS = 32


def partners(mask):
    return [(place, place ^ mask) for place in range(256)]


def groups_of(same):
    return [[place for place in range(256) if place & same == rest] for rest in range(256) if rest & same == rest]


def split(value):
    high = value.astype(BF16)
    low = (value - high.astype(F32)).astype(BF16)
    return high, low


def select(code_ref, square_ref):
    square_ref[...] = jnp.zeros((128, 128), F32)
    square_ref[: 2 * PAIRS, : code_ref.shape[1]] = code_ref[...].astype(F32)
    code = square_ref[...].T.astype(jnp.int32)
    labels = lax.broadcasted_iota(jnp.int32, (TILES, 128), 0)
    chosen = jnp.full((TILES, 128), -1, jnp.int32)
    for step in range(code_ref.shape[1]):
        row = code[step : step + 1, :]
        chosen = jnp.where(labels == (row & (TILES - 1)), row >> 6, chosen)
    return chosen.astype(F32)


def message_kernel(counts_ref, attenuation_ref, flux_ref, message0_ref, message1_ref, message2_ref, message3_ref, rows_ref):
    view = lax.axis_index("view")
    quarter = lax.axis_index("bin") ^ (2 * ((view >> 1) & 1))
    for v in range(4):
        for b in range(2):
            for s in range(0, 16, 8):
                piece = counts_ref[v, b, s : s + 8, :].astype(F32)
                piece = jnp.stack([piece[:, d * DEPTH : (d + 1) * DEPTH] for d in range(12)])
                row = b * PAIRS + v * 12
                rows_ref[s : s + 8, row : row + 12, :] = jnp.swapaxes(piece, 0, 1)
    refs = (message0_ref, message1_ref, message2_ref, message3_ref)
    for shift, ref in enumerate(refs):
        for s in range(4):
            piece = rows_ref[(quarter ^ shift) * 4 + s].astype(BF16)
            ref[: 2 * PAIRS, s * DEPTH : (s + 1) * DEPTH] = piece
    labels = lax.broadcasted_iota(jnp.int32, (8, DEPTH), 0)
    value = jnp.zeros((8, DEPTH), F32)
    for b in range(2):
        for m in range(4):
            figure = attenuation_ref[b, m] if m < 3 else flux_ref[b]
            value = jnp.where(labels == 4 * b + m, figure, value)
    first = value.astype(BF16)
    rest = value - first.astype(F32)
    second = rest.astype(BF16)
    third = (rest - second.astype(F32)).astype(BF16)
    upper = jnp.concatenate([first.astype(F32), second.astype(F32)], axis=1)
    lower = jnp.concatenate([third.astype(F32), jnp.zeros((8, DEPTH), F32)], axis=1)
    figures = jnp.concatenate([upper, lower], axis=0).astype(BF16)
    figures = jnp.concatenate([figures, figures], axis=1)
    for ref in refs:
        ref[2 * PAIRS :, :] = figures


def halves_kernel(mine_ref, theirs_ref, keep_ref, send_ref):
    first = lax.axis_index("view") & 1 == 0
    for far, ref in enumerate((mine_ref, theirs_ref)):
        rows = ref[...].astype(F32)
        parts = [jnp.concatenate([rows[m * 4 + 2 * c : m * 4 + 2 * c + 2] for m in range(3)], axis=0) for c in range(2)]
        keep_ref[far] = jnp.where(first, *parts).astype(BF16)
        send_ref[far] = jnp.where(first, *parts[::-1]).astype(BF16)


def forward_kernel(
    code_ref, volume_ref, basis_ref, mine_ref, theirs_ref, chosen_ref, rounded_ref, square_ref, rows_ref, parts_ref
):
    rows_ref[...] = volume_ref[...].astype(F32)
    volume = [rows_ref[:, near * CHANNELS + c, :].astype(BF16) for c in range(CHANNELS) for near in range(4)]
    volume = jnp.concatenate(volume, axis=0)
    for j in range(BANK // 2):
        both = jnp.concatenate([basis_ref[2 * j], basis_ref[2 * j + 1]], axis=1)
        table = jnp.dot(volume, both, preferred_element_type=F32)
        for part, value in enumerate(split(table)):
            for p in range(2):
                row = (part * BANK + 2 * j + p) * TILES
                for c in range(CHANNELS):
                    piece = value[c * TILES : (c + 1) * TILES, p * DEPTH : (p + 1) * DEPTH]
                    parts_ref[row : row + TILES, c * DEPTH : (c + 1) * DEPTH] = piece
    chosen = select(code_ref, square_ref)
    chosen_ref[...] = chosen
    part = (lax.broadcasted_iota(jnp.int32, (2 * PAIRS, 128), 1) // TILES).astype(F32)
    turned = jnp.concatenate([chosen, chosen], axis=0).T[: 2 * PAIRS] - part
    picks = [(turned == 2 * j).astype(F32).astype(BF16) for j in range(BANK // 2)]
    lines = jnp.dot(jnp.concatenate(picks * 2, axis=1), parts_ref[...], preferred_element_type=F32)

    line = [lines[:, m * SPAN : (m + 1) * SPAN] for m in range(3)]
    grads = [jnp.zeros((2 * PAIRS, SPAN), F32) for m in range(3)]
    for source in range(QUARTERS):
        figures = mine_ref[source, 2 * PAIRS :, :].astype(F32)
        figures = (figures[:8, :DEPTH] + figures[:8, DEPTH:]) + figures[8:, :DEPTH]
        figures = jnp.concatenate([figures] * 2, axis=1)
        for b in range(2):
            weight = [figures[4 * b + m : 4 * b + m + 1, :] for m in range(4)]
            exponent = weight[0] * line[0] + weight[1] * line[1] + weight[2] * line[2]
            photons = [ref[source, b * PAIRS : (b + 1) * PAIRS, :] for ref in (mine_ref, theirs_ref)]
            photons = jnp.concatenate(photons, axis=0).astype(F32)
            misfit = photons - weight[3] * jnp.exp(-exponent)
            grads = [grads[m] + weight[m] * misfit for m in range(3)]
    for m in range(3):
        rounded_ref[:, m * SPAN : (m + 1) * SPAN] = grads[m].astype(BF16)


def back_project(rounded, chosen_ref, basis_ref, parts_ref):
    own = [chosen_ref[far * 2 * SPOTS : far * 2 * SPOTS + SPOTS, : 2 * PAIRS] for far in range(2)]
    own = jnp.concatenate(own, axis=0)
    for j in range(BANK // 4):
        places = [(own == 4 * j + p).astype(F32).astype(BF16) for p in range(4)]
        summed = jnp.dot(jnp.concatenate(places, axis=0), rounded, preferred_element_type=F32)
        for part, value in enumerate(split(summed)):
            for p in range(4):
                col = (4 * j + p) * DEPTH
                for c in range(CHANNELS):
                    row = (part * CHANNELS + c) * HALF
                    piece = value[p * HALF : (p + 1) * HALF, c * DEPTH : (c + 1) * DEPTH]
                    parts_ref[row : row + HALF, col : col + DEPTH] = piece
    bank = jnp.concatenate([basis_ref[p] for p in range(BANK)], axis=1)
    turn = (((1,), (1,)), ((), ()))
    total = lax.dot_general(parts_ref[...], bank, turn, preferred_element_type=F32)
    return total[: CHANNELS * HALF] + total[CHANNELS * HALF :]


def own_kernel(rounded_ref, chosen_ref, basis_ref, total_ref, parts_ref):
    total_ref[...] = back_project(rounded_ref[...], chosen_ref, basis_ref, parts_ref)


def other_kernel(rounded_ref, chosen_ref, basis_ref, total_ref, grad_ref, parts_ref, rows_ref):
    rounded = jnp.concatenate([rounded_ref[PAIRS:], rounded_ref[:PAIRS]], axis=0)
    other = back_project(rounded, chosen_ref, basis_ref, parts_ref)
    own = total_ref[...]
    view = lax.axis_index("view")
    halves = jnp.where(view & 1 == 0, own, other), jnp.where(view & 1 == 0, other, own)
    lanes = lax.broadcasted_iota(jnp.int32, (SPOTS, WIDTH), 1)
    powers = jnp.zeros((SPOTS, WIDTH), F32)
    for core in range(2):
        for c in range(CHANNELS):
            pair = halves[core][c * HALF : (c + 1) * HALF]
            largest = jnp.max(jnp.abs(pair), axis=1, keepdims=True)
            power = jnp.ceil(jnp.log2(jnp.maximum(largest, 1e-30)) - 14.9)
            pair = jnp.floor(pair * jnp.exp2(-power) + 0.5)
            power = jnp.broadcast_to(power, (HALF, WIDTH))
            for far in range(2):
                row = far * BLOCK + core * CHANNELS + c
                rows_ref[:, row, :] = jnp.where(view & 2 == 2 * far, pair[:SPOTS], pair[SPOTS:])
                powers = jnp.where(lanes == row, jnp.where(view & 2 == 2 * far, power[:SPOTS], power[SPOTS:]), powers)
    for row in range(2 * BLOCK, ROWS):
        rows_ref[:, row, :] = powers
    grad_ref[...] = rows_ref[...].astype(jnp.int32).astype(jnp.int16)


def sum_kernel(scale, parts_ref, blocks_ref):
    total = jnp.zeros((2 * BLOCK, WIDTH), F32)
    shape = (2 * BLOCK, WIDTH)
    own = lax.broadcasted_iota(jnp.int32, shape, 0) == lax.broadcasted_iota(jnp.int32, shape, 1)
    for spot in range(SPOTS):
        part = parts_ref[spot].astype(jnp.int32).astype(F32)
        powers = jnp.broadcast_to(part[2 * BLOCK : 2 * BLOCK + 1], shape)
        power = jnp.sum(jnp.where(own, powers, 0.0), axis=1, keepdims=True)
        total += part[: 2 * BLOCK] * jnp.exp2(power)
    total = total * scale
    for place in range(2 * QUARTERS):
        blocks_ref[place] = total[:BLOCK] if place < QUARTERS else total[BLOCK:]


FORWARD = [
    pltpu.VMEM((128, 128), F32),
    pltpu.VMEM((SPOTS, 2 * BLOCK, WIDTH), F32),
    pltpu.VMEM((2 * BANK * TILES, CHANNELS * DEPTH), BF16),
]
BACKWARD = [pltpu.VMEM((2 * CHANNELS * HALF, BANK * DEPTH), BF16)]


def call(kernel, out_shape, scratch, *operands):
    vmem = pl.BlockSpec(memory_space=pltpu.VMEM)
    return pl.pallas_call(
        kernel,
        out_shape=out_shape,
        in_specs=[vmem] * len(operands),
        out_specs=jax.tree.map(lambda _: vmem, out_shape),
        scratch_shapes=scratch,
        compiler_params=pltpu.CompilerParams(vmem_limit_bytes=32 * 2**20),
    )(*operands)


def on_device(volume, basis, tile_index, tile_offset, attenuation, flux, counts):
    view = lax.axis_index("view")
    core = view & 1
    far = (view >> 1) & 1
    quarter = lax.axis_index("bin") ^ (2 * far)
    views, det_tiles, band = tile_index.shape
    slices = volume.shape[2]
    plane_groups = groups_of(PLANE)
    line_groups = groups_of(255 ^ LINE)

    mine = lax.dynamic_slice_in_dim(volume[0], quarter * 4, 4, 1).reshape(2 * CHANNELS, WIDTH)
    theirs = lax.ppermute(mine, BOTH, partners(FAR))

    vmem = pl.BlockSpec(memory_space=pltpu.VMEM)
    smem = pl.BlockSpec(memory_space=pltpu.SMEM)
    messages = pl.pallas_call(
        message_kernel,
        out_shape=[jax.ShapeDtypeStruct((2 * PAIRS + 16, 2 * SPAN), BF16)] * QUARTERS,
        in_specs=[vmem, smem, smem],
        out_specs=[vmem] * QUARTERS,
        scratch_shapes=[pltpu.VMEM((16, 2 * PAIRS, DEPTH), F32)],
        compiler_params=pltpu.CompilerParams(vmem_limit_bytes=8 * 2**20),
    )(counts, attenuation, flux)

    mine, theirs = pl.pallas_call(
        halves_kernel,
        out_shape=[jax.ShapeDtypeStruct((2, CHANNELS, WIDTH), BF16)] * 2,
        in_specs=[vmem] * 2,
        out_specs=[vmem] * 2,
        compiler_params=pltpu.CompilerParams(vmem_limit_bytes=4 * 2**20),
        cost_estimate=pl.CostEstimate(flops=0, bytes_accessed=10**8, transcendentals=0),
    )(mine, theirs)
    theirs = lax.ppermute(theirs, BOTH, partners(CORE))
    stack = jnp.stack([mine, theirs], axis=1)
    stack = jnp.broadcast_to(stack.reshape(1, 2 * BLOCK, WIDTH), (SPOTS, 2 * BLOCK, WIDTH))
    tiles = lax.all_to_all(stack, BOTH, 0, 0, tiled=True, axis_index_groups=plane_groups)

    arrived = [lax.ppermute(messages[shift], BOTH, partners(shift)) for shift in (3, 2, 1)] + [messages[0]]
    arrived = jnp.stack(arrived)
    keep = lax.dynamic_slice_in_dim(arrived, core * SPAN, SPAN, 2)
    other = lax.dynamic_slice_in_dim(arrived[:, : 2 * PAIRS], (1 - core) * SPAN, SPAN, 2)

    code = tile_index.reshape(PAIRS, band) + TILES * tile_offset.reshape(PAIRS, band)
    other, code = lax.optimization_barrier((other, code))
    other = lax.ppermute(other, BOTH, partners(CORE))
    code = jnp.concatenate([code, lax.ppermute(code, BOTH, partners(CORE))], axis=0)
    index = (code & (TILES - 1)) ^ (view & 3)
    index = ((index >> 1) & 1) * 2 * SPOTS + (index & 1) * SPOTS + (index >> 2)
    code = index | (code & -TILES)

    wide = CHANNELS * DEPTH
    chosen, rounded = call(
        forward_kernel,
        [jax.ShapeDtypeStruct((TILES, 128), F32), jax.ShapeDtypeStruct((2 * PAIRS, wide), BF16)],
        FORWARD,
        code,
        tiles,
        basis,
        keep,
        other,
    )
    swapped = lax.ppermute(rounded, BOTH, partners(CORE))
    total = call(
        own_kernel, jax.ShapeDtypeStruct((CHANNELS * HALF, WIDTH), F32), BACKWARD, rounded, chosen, basis
    )
    grads = call(
        other_kernel,
        jax.ShapeDtypeStruct((SPOTS, ROWS, WIDTH), jnp.int16),
        BACKWARD + [pltpu.VMEM((SPOTS, ROWS, WIDTH), F32)],
        swapped,
        chosen,
        basis,
        total,
    )

    parts = lax.all_to_all(grads, BOTH, 0, 0, tiled=True, axis_index_groups=plane_groups)
    scale = 1.0 / (8.0 * math.sqrt(views * lax.axis_size("view")))
    blocks = pl.pallas_call(
        functools.partial(sum_kernel, scale),
        out_shape=jax.ShapeDtypeStruct((2 * QUARTERS, BLOCK, WIDTH), F32),
        in_specs=[vmem],
        out_specs=vmem,
        compiler_params=pltpu.CompilerParams(vmem_limit_bytes=8 * 2**20),
    )(parts)
    blocks = lax.all_to_all(blocks, BOTH, 0, 0, tiled=True, axis_index_groups=line_groups)
    quarters = blocks[:4] + jnp.concatenate([blocks[6:], blocks[4:6]], axis=0)
    quarters = quarters.reshape(QUARTERS, 2, 3, 2, WIDTH).transpose(2, 0, 1, 3, 4)
    return quarters.reshape(1, 3, slices, WIDTH)


def solution(mesh):
    placed = (
        P("view", None, None, None),
        P(),
        P("view", None, None),
        P("view", None, None),
        P("bin", None),
        P("bin"),
        P("view", "bin", None, None),
    )
    return jax.shard_map(
        on_device,
        mesh=mesh,
        in_specs=placed,
        out_specs=P("view", None, None, None),
        check_vma=False,
    )
```

```python
import functools
import math

import jax
import jax.numpy as jnp
from jax import lax
from jax.experimental import pallas as pl
from jax.experimental.pallas import tpu as pltpu
from jax.sharding import PartitionSpec as P

BOTH = ("view", "bin")
BF16 = jnp.bfloat16
F32 = jnp.float32

CORE = 4
FAR = 8 + 2
PLANE = 15
LINE = 11

SPOTS = 16
HALF = 32
HALF = 32
TILES = 64
QUARTERS = 4
CHANNELS = 6
PAIRS = 48
BANK = 16
WIDTH = 256
DEPTH = 128
SPAN = 2 * DEPTH
BLOCK = 2 * CHANNELS
ROWS = 4 * BLOCK + 8


def partners(mask):
    return [(place, place ^ mask) for place in range(256)]


def groups_of(same):
    return [[place for place in range(256) if place & same == rest] for rest in range(256) if rest & same == rest]


def split(value):
    high = value.astype(BF16)
    low = (value - high.astype(F32)).astype(BF16)
    return high, low


def select(code_ref, square_ref):
    square_ref[...] = jnp.zeros((128, 128), F32)
    square_ref[: 2 * PAIRS, : code_ref.shape[1]] = code_ref[...].astype(F32)
    code = square_ref[...].T.astype(jnp.int32)
    labels = lax.broadcasted_iota(jnp.int32, (TILES, 128), 0)
    chosen = jnp.full((TILES, 128), -1, jnp.int32)
    for step in range(code_ref.shape[1]):
        row = code[step : step + 1, :]
        chosen = jnp.where(labels == (row & (TILES - 1)), row >> 6, chosen)
    return chosen.astype(F32)


def prepare_kernel(code_ref, basis_ref, chosen_ref, picks_ref, bank_ref, square_ref):
    chosen = select(code_ref, square_ref)
    chosen_ref[...] = chosen
    part = (lax.broadcasted_iota(jnp.int32, (2 * PAIRS, 128), 1) // TILES).astype(F32)
    turned = jnp.concatenate([chosen, chosen], axis=0).T[: 2 * PAIRS] - part
    for j in range(BANK // 2):
        pick = (turned == 2 * j).astype(F32).astype(BF16)
        for half in range(2):
            col = (half * BANK // 2 + j) * 128
            picks_ref[:, col : col + 128] = pick
    for p in range(BANK):
        bank_ref[p * DEPTH : (p + 1) * DEPTH, :] = basis_ref[p].T


def message_kernel(counts_ref, attenuation_ref, flux_ref, message0_ref, message1_ref, message2_ref, message3_ref, rows_ref):
    view = lax.axis_index("view")
    quarter = lax.axis_index("bin") ^ (2 * ((view >> 1) & 1))
    for v in range(4):
        for b in range(2):
            for s in range(0, 16, 8):
                piece = counts_ref[v, b, s : s + 8, :].astype(F32)
                piece = jnp.stack([piece[:, d * DEPTH : (d + 1) * DEPTH] for d in range(12)])
                row = b * PAIRS + v * 12
                rows_ref[s : s + 8, row : row + 12, :] = jnp.swapaxes(piece, 0, 1)
    refs = (message0_ref, message1_ref, message2_ref, message3_ref)
    for shift, ref in enumerate(refs):
        for s in range(4):
            piece = rows_ref[(quarter ^ shift) * 4 + s].astype(BF16)
            ref[: 2 * PAIRS, s * DEPTH : (s + 1) * DEPTH] = piece
    labels = lax.broadcasted_iota(jnp.int32, (8, DEPTH), 0)
    value = jnp.zeros((8, DEPTH), F32)
    for b in range(2):
        for m in range(4):
            figure = attenuation_ref[b, m] if m < 3 else flux_ref[b]
            value = jnp.where(labels == 4 * b + m, figure, value)
    first = value.astype(BF16)
    rest = value - first.astype(F32)
    second = rest.astype(BF16)
    third = (rest - second.astype(F32)).astype(BF16)
    upper = jnp.concatenate([first.astype(F32), second.astype(F32)], axis=1)
    lower = jnp.concatenate([third.astype(F32), jnp.zeros((8, DEPTH), F32)], axis=1)
    figures = jnp.concatenate([upper, lower], axis=0).astype(BF16)
    figures = jnp.concatenate([figures, figures], axis=1)
    for ref in refs:
        ref[2 * PAIRS :, :] = figures


def halves_kernel(mine_ref, theirs_ref, keep_ref, send_ref):
    first = lax.axis_index("view") & 1 == 0
    for far, ref in enumerate((mine_ref, theirs_ref)):
        rows = ref[...].astype(F32)
        parts = [jnp.concatenate([rows[m * 4 + 2 * c : m * 4 + 2 * c + 2] for m in range(3)], axis=0) for c in range(2)]
        keep_ref[far] = jnp.where(first, *parts).astype(BF16)
        send_ref[far] = jnp.where(first, *parts[::-1]).astype(BF16)


def forward_kernel(
    picks_ref, volume_ref, basis_ref, mine_ref, theirs_ref, rounded_ref, rows_ref, parts_ref
):
    rows_ref[...] = volume_ref[...].astype(F32)
    volume = [rows_ref[:, near * CHANNELS + c, :].astype(BF16) for c in range(CHANNELS) for near in range(4)]
    volume = jnp.concatenate(volume, axis=0)
    for j in range(BANK // 2):
        both = jnp.concatenate([basis_ref[2 * j], basis_ref[2 * j + 1]], axis=1)
        table = jnp.dot(volume, both, preferred_element_type=F32)
        for part, value in enumerate(split(table)):
            for p in range(2):
                row = (part * BANK + 2 * j + p) * TILES
                for c in range(CHANNELS):
                    piece = value[c * TILES : (c + 1) * TILES, p * DEPTH : (p + 1) * DEPTH]
                    parts_ref[row : row + TILES, c * DEPTH : (c + 1) * DEPTH] = piece
    lines = jnp.dot(picks_ref[...], parts_ref[...], preferred_element_type=F32)

    line = [lines[:, m * SPAN : (m + 1) * SPAN] for m in range(3)]
    grads = [jnp.zeros((2 * PAIRS, SPAN), F32) for m in range(3)]
    for source in range(QUARTERS):
        figures = mine_ref[source, 2 * PAIRS :, :].astype(F32)
        figures = (figures[:8, :DEPTH] + figures[:8, DEPTH:]) + figures[8:, :DEPTH]
        figures = jnp.concatenate([figures] * 2, axis=1)
        for b in range(2):
            weight = [figures[4 * b + m : 4 * b + m + 1, :] for m in range(4)]
            exponent = weight[0] * line[0] + weight[1] * line[1] + weight[2] * line[2]
            photons = [ref[source, b * PAIRS : (b + 1) * PAIRS, :] for ref in (mine_ref, theirs_ref)]
            photons = jnp.concatenate(photons, axis=0).astype(F32)
            misfit = photons - weight[3] * jnp.exp(-exponent)
            grads = [grads[m] + weight[m] * misfit for m in range(3)]
    for m in range(3):
        rounded_ref[:, m * SPAN : (m + 1) * SPAN] = grads[m].astype(BF16)


def back_project(rounded, chosen_ref, bank_ref, parts_ref):
    own = [chosen_ref[far * 2 * SPOTS : far * 2 * SPOTS + SPOTS, : 2 * PAIRS] for far in range(2)]
    own = jnp.concatenate(own, axis=0)
    for j in range(BANK // 4):
        places = [(own == 4 * j + p).astype(F32).astype(BF16) for p in range(4)]
        summed = jnp.dot(jnp.concatenate(places, axis=0), rounded, preferred_element_type=F32)
        for part, value in enumerate(split(summed)):
            for p in range(4):
                col = (4 * j + p) * DEPTH
                for c in range(CHANNELS):
                    row = (part * CHANNELS + c) * HALF
                    piece = value[p * HALF : (p + 1) * HALF, c * DEPTH : (c + 1) * DEPTH]
                    parts_ref[row : row + HALF, col : col + DEPTH] = piece
    total = jnp.dot(parts_ref[...], bank_ref[...], preferred_element_type=F32)
    return total[: CHANNELS * HALF] + total[CHANNELS * HALF :]


def own_kernel(rounded_ref, chosen_ref, bank_ref, total_ref, parts_ref):
    total_ref[...] = back_project(rounded_ref[...], chosen_ref, bank_ref, parts_ref)


def other_kernel(rounded_ref, chosen_ref, bank_ref, total_ref, grad_ref, parts_ref, rows_ref):
    rounded = jnp.concatenate([rounded_ref[PAIRS:], rounded_ref[:PAIRS]], axis=0)
    other = back_project(rounded, chosen_ref, bank_ref, parts_ref)
    own = total_ref[...]
    view = lax.axis_index("view")
    halves = jnp.where(view & 1 == 0, own, other), jnp.where(view & 1 == 0, other, own)
    lanes = lax.broadcasted_iota(jnp.int32, (SPOTS, 128), 1)
    powers = jnp.zeros((SPOTS, 128), F32)
    for core in range(2):
        for c in range(CHANNELS):
            pair = halves[core][c * HALF : (c + 1) * HALF]
            largest = jnp.max(jnp.abs(pair), axis=1, keepdims=True)
            power = jnp.ceil(jnp.log2(jnp.maximum(largest, 1e-30)) - 14.9)
            pair = jnp.floor(pair * jnp.exp2(-power) + 0.5)
            power = jnp.broadcast_to(power, (HALF, 128))
            for far in range(2):
                row = far * BLOCK + core * CHANNELS + c
                tile = jnp.where(view & 2 == 2 * far, pair[:SPOTS], pair[SPOTS:])
                rows_ref[:, row, :] = tile[:, :128]
                rows_ref[:, 2 * BLOCK + row, :] = tile[:, 128:]
                powers = jnp.where(lanes == row, jnp.where(view & 2 == 2 * far, power[:SPOTS], power[SPOTS:]), powers)
    for row in range(4 * BLOCK, ROWS):
        rows_ref[:, row, :] = powers
    grad_ref[...] = rows_ref[...].astype(jnp.int32).astype(jnp.int16)


def sum_kernel(scale, parts_ref, blocks_ref):
    total = jnp.zeros((2 * BLOCK, WIDTH), F32)
    shape = (2 * BLOCK, 128)
    own = lax.broadcasted_iota(jnp.int32, shape, 0) == lax.broadcasted_iota(jnp.int32, shape, 1)
    for spot in range(SPOTS):
        part = parts_ref[spot].astype(jnp.int32).astype(F32)
        powers = jnp.broadcast_to(part[4 * BLOCK : 4 * BLOCK + 1], shape)
        power = jnp.sum(jnp.where(own, powers, 0.0), axis=1, keepdims=True)
        part = jnp.concatenate([part[: 2 * BLOCK], part[2 * BLOCK : 4 * BLOCK]], axis=1)
        total += part * jnp.exp2(power)
    total = total * scale
    for place in range(2 * QUARTERS):
        blocks_ref[place] = total[:BLOCK] if place < QUARTERS else total[BLOCK:]


FORWARD = [
    pltpu.VMEM((SPOTS, 2 * BLOCK, WIDTH), F32),
    pltpu.VMEM((2 * BANK * TILES, CHANNELS * DEPTH), BF16),
]
BACKWARD = [pltpu.VMEM((2 * CHANNELS * HALF, BANK * DEPTH), BF16)]


def call(kernel, out_shape, scratch, *operands):
    vmem = pl.BlockSpec(memory_space=pltpu.VMEM)
    return pl.pallas_call(
        kernel,
        out_shape=out_shape,
        in_specs=[vmem] * len(operands),
        out_specs=jax.tree.map(lambda _: vmem, out_shape),
        scratch_shapes=scratch,
        compiler_params=pltpu.CompilerParams(vmem_limit_bytes=32 * 2**20),
    )(*operands)


def on_device(volume, basis, tile_index, tile_offset, attenuation, flux, counts):
    view = lax.axis_index("view")
    core = view & 1
    far = (view >> 1) & 1
    quarter = lax.axis_index("bin") ^ (2 * far)
    views, det_tiles, band = tile_index.shape
    slices = volume.shape[2]
    plane_groups = groups_of(PLANE)
    line_groups = groups_of(255 ^ LINE)

    mine = lax.dynamic_slice_in_dim(volume[0], quarter * 4, 4, 1).reshape(2 * CHANNELS, WIDTH)
    theirs = lax.ppermute(mine, BOTH, partners(FAR))

    vmem = pl.BlockSpec(memory_space=pltpu.VMEM)
    smem = pl.BlockSpec(memory_space=pltpu.SMEM)
    messages = pl.pallas_call(
        message_kernel,
        out_shape=[jax.ShapeDtypeStruct((2 * PAIRS + 16, 2 * SPAN), BF16)] * QUARTERS,
        in_specs=[vmem, smem, smem],
        out_specs=[vmem] * QUARTERS,
        scratch_shapes=[pltpu.VMEM((16, 2 * PAIRS, DEPTH), F32)],
        compiler_params=pltpu.CompilerParams(vmem_limit_bytes=8 * 2**20),
    )(counts, attenuation, flux)

    mine, theirs = pl.pallas_call(
        halves_kernel,
        out_shape=[jax.ShapeDtypeStruct((2, CHANNELS, WIDTH), BF16)] * 2,
        in_specs=[vmem] * 2,
        out_specs=[vmem] * 2,
        compiler_params=pltpu.CompilerParams(vmem_limit_bytes=4 * 2**20),
        cost_estimate=pl.CostEstimate(flops=0, bytes_accessed=10**8, transcendentals=0),
    )(mine, theirs)
    theirs = lax.ppermute(theirs, BOTH, partners(CORE))
    stack = jnp.stack([mine, theirs], axis=1)
    stack = jnp.broadcast_to(stack.reshape(1, 2 * BLOCK, WIDTH), (SPOTS, 2 * BLOCK, WIDTH))
    tiles = lax.all_to_all(stack, BOTH, 0, 0, tiled=True, axis_index_groups=plane_groups)

    arrived = [lax.ppermute(messages[shift], BOTH, partners(shift)) for shift in (3, 2, 1)] + [messages[0]]
    arrived = jnp.stack(arrived)
    keep = lax.dynamic_slice_in_dim(arrived, core * SPAN, SPAN, 2)
    other = lax.dynamic_slice_in_dim(arrived[:, : 2 * PAIRS], (1 - core) * SPAN, SPAN, 2)

    code = tile_index.reshape(PAIRS, band) + TILES * tile_offset.reshape(PAIRS, band)
    other, code = lax.optimization_barrier((other, code))
    other = lax.ppermute(other, BOTH, partners(CORE))
    code = jnp.concatenate([code, lax.ppermute(code, BOTH, partners(CORE))], axis=0)
    index = (code & (TILES - 1)) ^ (view & 3)
    index = ((index >> 1) & 1) * 2 * SPOTS + (index & 1) * SPOTS + (index >> 2)
    code = index | (code & -TILES)

    wide = CHANNELS * DEPTH
    chosen, picks, bank = pl.pallas_call(
        prepare_kernel,
        out_shape=[
            jax.ShapeDtypeStruct((TILES, 128), F32),
            jax.ShapeDtypeStruct((2 * PAIRS, 2 * BANK * TILES), BF16),
            jax.ShapeDtypeStruct((BANK * DEPTH, WIDTH), BF16),
        ],
        in_specs=[vmem] * 2,
        out_specs=[vmem] * 3,
        scratch_shapes=[pltpu.VMEM((128, 128), F32)],
        compiler_params=pltpu.CompilerParams(vmem_limit_bytes=8 * 2**20),
    )(code, basis)
    rounded = call(
        forward_kernel,
        jax.ShapeDtypeStruct((2 * PAIRS, wide), BF16),
        FORWARD,
        picks,
        tiles,
        basis,
        keep,
        other,
    )
    swapped = lax.ppermute(rounded, BOTH, partners(CORE))
    total = call(
        own_kernel, jax.ShapeDtypeStruct((CHANNELS * HALF, WIDTH), F32), BACKWARD, rounded, chosen, bank
    )
    grads = call(
        other_kernel,
        jax.ShapeDtypeStruct((SPOTS, ROWS, 128), jnp.int16),
        BACKWARD + [pltpu.VMEM((SPOTS, ROWS, 128), F32)],
        swapped,
        chosen,
        bank,
        total,
    )

    parts = lax.all_to_all(grads, BOTH, 0, 0, tiled=True, axis_index_groups=plane_groups)
    scale = 1.0 / (8.0 * math.sqrt(views * lax.axis_size("view")))
    blocks = pl.pallas_call(
        functools.partial(sum_kernel, scale),
        out_shape=jax.ShapeDtypeStruct((2 * QUARTERS, BLOCK, WIDTH), F32),
        in_specs=[vmem],
        out_specs=vmem,
        compiler_params=pltpu.CompilerParams(vmem_limit_bytes=8 * 2**20),
    )(parts)
    blocks = lax.all_to_all(blocks, BOTH, 0, 0, tiled=True, axis_index_groups=line_groups)
    quarters = blocks[:4] + jnp.concatenate([blocks[6:], blocks[4:6]], axis=0)
    quarters = quarters.reshape(QUARTERS, 2, 3, 2, WIDTH).transpose(2, 0, 1, 3, 4)
    return quarters.reshape(1, 3, slices, WIDTH)


def solution(mesh):
    placed = (
        P("view", None, None, None),
        P(),
        P("view", None, None),
        P("view", None, None),
        P("bin", None),
        P("bin"),
        P("view", "bin", None, None),
    )
    return jax.shard_map(
        on_device,
        mesh=mesh,
        in_specs=placed,
        out_specs=P("view", None, None, None),
        check_vma=False,
    )
```

```python
import functools
import math

import jax
import jax.numpy as jnp
from jax import lax
from jax.experimental import pallas as pl
from jax.experimental.pallas import tpu as pltpu
from jax.sharding import PartitionSpec as P

BOTH = ("view", "bin")
BF16 = jnp.bfloat16
F32 = jnp.float32

CORE = 4
FAR = 8 + 2
PLANE = 15
LINE = 11

SPOTS = 16
HALF = 32
HALF = 32
TILES = 64
QUARTERS = 4
CHANNELS = 6
PAIRS = 48
BANK = 16
WIDTH = 256
DEPTH = 128
SPAN = 2 * DEPTH
BLOCK = 2 * CHANNELS
ROWS = 4 * BLOCK + 8


def partners(mask):
    return [(place, place ^ mask) for place in range(256)]


def groups_of(same):
    return [[place for place in range(256) if place & same == rest] for rest in range(256) if rest & same == rest]


def split(value):
    high = value.astype(BF16)
    low = (value - high.astype(F32)).astype(BF16)
    return high, low


def select(code_ref, square_ref):
    square_ref[...] = jnp.zeros((128, 128), F32)
    square_ref[: 2 * PAIRS, : code_ref.shape[1]] = code_ref[...].astype(F32)
    code = square_ref[...].T.astype(jnp.int32)
    labels = lax.broadcasted_iota(jnp.int32, (TILES, 128), 0)
    chosen = jnp.full((TILES, 128), -1, jnp.int32)
    for step in range(code_ref.shape[1]):
        row = code[step : step + 1, :]
        chosen = jnp.where(labels == (row & (TILES - 1)), row >> 6, chosen)
    return chosen.astype(F32)


def prepare_kernel(code_ref, basis_ref, chosen_ref, picks_ref, bank_ref, square_ref):
    chosen = select(code_ref, square_ref)
    chosen_ref[...] = chosen
    part = (lax.broadcasted_iota(jnp.int32, (2 * PAIRS, 128), 1) // TILES).astype(F32)
    turned = jnp.concatenate([chosen, chosen], axis=0).T[: 2 * PAIRS] - part
    for j in range(BANK // 2):
        pick = (turned == 2 * j).astype(F32).astype(BF16)
        for half in range(2):
            col = (half * BANK // 2 + j) * 128
            picks_ref[:, col : col + 128] = pick
    for p in range(BANK):
        bank_ref[p * DEPTH : (p + 1) * DEPTH, :] = basis_ref[p].T


def message_kernel(counts_ref, attenuation_ref, flux_ref, message0_ref, message1_ref, message2_ref, message3_ref, rows_ref):
    view = lax.axis_index("view")
    quarter = lax.axis_index("bin") ^ (2 * ((view >> 1) & 1))
    for v in range(4):
        for b in range(2):
            for s in range(0, 16, 8):
                piece = counts_ref[v, b, s : s + 8, :].astype(F32)
                piece = jnp.stack([piece[:, d * DEPTH : (d + 1) * DEPTH] for d in range(12)])
                row = b * PAIRS + v * 12
                rows_ref[s : s + 8, row : row + 12, :] = jnp.swapaxes(piece, 0, 1)
    refs = (message0_ref, message1_ref, message2_ref, message3_ref)
    for shift, ref in enumerate(refs):
        for s in range(4):
            piece = rows_ref[(quarter ^ shift) * 4 + s].astype(BF16)
            ref[: 2 * PAIRS, s * DEPTH : (s + 1) * DEPTH] = piece
    labels = lax.broadcasted_iota(jnp.int32, (8, DEPTH), 0)
    value = jnp.zeros((8, DEPTH), F32)
    for b in range(2):
        for m in range(4):
            figure = attenuation_ref[b, m] if m < 3 else flux_ref[b]
            value = jnp.where(labels == 4 * b + m, figure, value)
    first = value.astype(BF16)
    rest = value - first.astype(F32)
    second = rest.astype(BF16)
    third = (rest - second.astype(F32)).astype(BF16)
    upper = jnp.concatenate([first.astype(F32), second.astype(F32)], axis=1)
    lower = jnp.concatenate([third.astype(F32), jnp.zeros((8, DEPTH), F32)], axis=1)
    figures = jnp.concatenate([upper, lower], axis=0).astype(BF16)
    figures = jnp.concatenate([figures, figures], axis=1)
    for ref in refs:
        ref[2 * PAIRS :, :] = figures


def halves_kernel(mine_ref, theirs_ref, keep_ref, send_ref):
    first = lax.axis_index("view") & 1 == 0
    for far, ref in enumerate((mine_ref, theirs_ref)):
        rows = ref[...].astype(F32)
        parts = [jnp.concatenate([rows[m * 4 + 2 * c : m * 4 + 2 * c + 2] for m in range(3)], axis=0) for c in range(2)]
        keep_ref[far] = jnp.where(first, *parts).astype(BF16)
        send_ref[far] = jnp.where(first, *parts[::-1]).astype(BF16)


def forward_kernel(
    picks_ref, volume_ref, basis_ref, mine_ref, theirs_ref, rounded_ref, rows_ref, parts_ref
):
    rows_ref[...] = volume_ref[...].astype(F32)
    volume = [rows_ref[:, near * CHANNELS + c, :].astype(BF16) for c in range(CHANNELS) for near in range(4)]
    volume = jnp.concatenate(volume, axis=0)
    for j in range(BANK // 2):
        both = jnp.concatenate([basis_ref[2 * j], basis_ref[2 * j + 1]], axis=1)
        table = jnp.dot(volume, both, preferred_element_type=F32)
        for part, value in enumerate(split(table)):
            for p in range(2):
                row = (part * BANK + 2 * j + p) * TILES
                for c in range(CHANNELS):
                    piece = value[c * TILES : (c + 1) * TILES, p * DEPTH : (p + 1) * DEPTH]
                    parts_ref[row : row + TILES, c * DEPTH : (c + 1) * DEPTH] = piece
    lines = jnp.dot(picks_ref[...], parts_ref[...], preferred_element_type=F32)

    line = [lines[:, m * SPAN : (m + 1) * SPAN] for m in range(3)]
    grads = [jnp.zeros((2 * PAIRS, SPAN), F32) for m in range(3)]
    for source in range(QUARTERS):
        figures = mine_ref[source, 2 * PAIRS :, :].astype(F32)
        figures = (figures[:8, :DEPTH] + figures[:8, DEPTH:]) + figures[8:, :DEPTH]
        figures = jnp.concatenate([figures] * 2, axis=1)
        for b in range(2):
            weight = [figures[4 * b + m : 4 * b + m + 1, :] for m in range(4)]
            exponent = weight[0] * line[0] + weight[1] * line[1] + weight[2] * line[2]
            photons = [ref[source, b * PAIRS : (b + 1) * PAIRS, :] for ref in (mine_ref, theirs_ref)]
            photons = jnp.concatenate(photons, axis=0).astype(F32)
            misfit = photons - weight[3] * jnp.exp(-exponent)
            grads = [grads[m] + weight[m] * misfit for m in range(3)]
    for m in range(3):
        rounded_ref[:, m * SPAN : (m + 1) * SPAN] = grads[m].astype(BF16)


def back_project(rounded, chosen_ref, bank_ref, parts_ref):
    own = [chosen_ref[far * 2 * SPOTS : far * 2 * SPOTS + SPOTS, : 2 * PAIRS] for far in range(2)]
    own = jnp.concatenate(own, axis=0)
    for j in range(BANK // 4):
        places = [(own == 4 * j + p).astype(F32).astype(BF16) for p in range(4)]
        summed = jnp.dot(jnp.concatenate(places, axis=0), rounded, preferred_element_type=F32)
        for part, value in enumerate(split(summed)):
            for p in range(4):
                col = (4 * j + p) * DEPTH
                for c in range(CHANNELS):
                    row = (part * CHANNELS + c) * HALF
                    piece = value[p * HALF : (p + 1) * HALF, c * DEPTH : (c + 1) * DEPTH]
                    parts_ref[row : row + HALF, col : col + DEPTH] = piece
    total = jnp.dot(parts_ref[...], bank_ref[...], preferred_element_type=F32)
    return total[: CHANNELS * HALF] + total[CHANNELS * HALF :]


def encode(pair):
    largest = jnp.max(jnp.abs(pair), axis=1, keepdims=True)
    power = jnp.ceil(jnp.log2(jnp.maximum(largest, 1e-30)) - 14.9)
    return jnp.floor(pair * jnp.exp2(-power) + 0.5), jnp.broadcast_to(power, (pair.shape[0], 128))


def own_kernel(rounded_ref, chosen_ref, bank_ref, total_ref, power_ref, parts_ref):
    total = back_project(rounded_ref[...], chosen_ref, bank_ref, parts_ref)
    total_ref[...], power_ref[...] = encode(total)


def other_kernel(rounded_ref, chosen_ref, bank_ref, total_ref, power_ref, grad_ref, parts_ref, rows_ref):
    rounded = jnp.concatenate([rounded_ref[PAIRS:], rounded_ref[:PAIRS]], axis=0)
    other, other_power = encode(back_project(rounded, chosen_ref, bank_ref, parts_ref))
    lanes = lax.broadcasted_iota(jnp.int32, (SPOTS, 128), 1)
    powers = jnp.zeros((SPOTS, 128), F32)
    for half, (total, power) in enumerate(((total_ref[...], power_ref[...]), (other, other_power))):
        for c in range(CHANNELS):
            for far in range(2):
                place = c * HALF + far * SPOTS
                row = far * BLOCK + half * CHANNELS + c
                rows_ref[:, row, :] = total[place : place + SPOTS, :128]
                rows_ref[:, 2 * BLOCK + row, :] = total[place : place + SPOTS, 128:]
                powers = jnp.where(lanes == row, power[place : place + SPOTS], powers)
    for row in range(4 * BLOCK, ROWS):
        rows_ref[:, row, :] = powers
    grad_ref[...] = rows_ref[...].astype(jnp.int32).astype(jnp.int16)


def sum_kernel(scale, parts_ref, blocks_ref):
    total = jnp.zeros((2 * BLOCK, WIDTH), F32)
    shape = (2 * BLOCK, 128)
    own = lax.broadcasted_iota(jnp.int32, shape, 0) == lax.broadcasted_iota(jnp.int32, shape, 1)
    for spot in range(SPOTS):
        part = parts_ref[spot].astype(jnp.int32).astype(F32)
        powers = jnp.broadcast_to(part[4 * BLOCK : 4 * BLOCK + 1], shape)
        power = jnp.sum(jnp.where(own, powers, 0.0), axis=1, keepdims=True)
        part = jnp.concatenate([part[: 2 * BLOCK], part[2 * BLOCK : 4 * BLOCK]], axis=1)
        total += part * jnp.exp2(power)
    total = total * scale
    view = lax.axis_index("view")
    tiles = []
    for far in range(2):
        own, other = [total[far * BLOCK + h * CHANNELS : far * BLOCK + (h + 1) * CHANNELS] for h in range(2)]
        first = view & 1 == 0
        tiles.append(jnp.concatenate([jnp.where(first, own, other), jnp.where(first, other, own)], axis=0))
    near = view & 2 == 0
    tiles = jnp.where(near, *tiles), jnp.where(near, *tiles[::-1])
    for place in range(2 * QUARTERS):
        blocks_ref[place] = tiles[place // QUARTERS]


FORWARD = [
    pltpu.VMEM((SPOTS, 2 * BLOCK, WIDTH), F32),
    pltpu.VMEM((2 * BANK * TILES, CHANNELS * DEPTH), BF16),
]
BACKWARD = [pltpu.VMEM((2 * CHANNELS * HALF, BANK * DEPTH), BF16)]


def call(kernel, out_shape, scratch, *operands):
    vmem = pl.BlockSpec(memory_space=pltpu.VMEM)
    return pl.pallas_call(
        kernel,
        out_shape=out_shape,
        in_specs=[vmem] * len(operands),
        out_specs=jax.tree.map(lambda _: vmem, out_shape),
        scratch_shapes=scratch,
        compiler_params=pltpu.CompilerParams(vmem_limit_bytes=32 * 2**20),
    )(*operands)


def on_device(volume, basis, tile_index, tile_offset, attenuation, flux, counts):
    view = lax.axis_index("view")
    core = view & 1
    far = (view >> 1) & 1
    quarter = lax.axis_index("bin") ^ (2 * far)
    views, det_tiles, band = tile_index.shape
    slices = volume.shape[2]
    plane_groups = groups_of(PLANE)
    line_groups = groups_of(255 ^ LINE)

    mine = lax.dynamic_slice_in_dim(volume[0], quarter * 4, 4, 1).reshape(2 * CHANNELS, WIDTH)
    theirs = lax.ppermute(mine, BOTH, partners(FAR))

    vmem = pl.BlockSpec(memory_space=pltpu.VMEM)
    smem = pl.BlockSpec(memory_space=pltpu.SMEM)
    messages = pl.pallas_call(
        message_kernel,
        out_shape=[jax.ShapeDtypeStruct((2 * PAIRS + 16, 2 * SPAN), BF16)] * QUARTERS,
        in_specs=[vmem, smem, smem],
        out_specs=[vmem] * QUARTERS,
        scratch_shapes=[pltpu.VMEM((16, 2 * PAIRS, DEPTH), F32)],
        compiler_params=pltpu.CompilerParams(vmem_limit_bytes=8 * 2**20),
    )(counts, attenuation, flux)

    mine, theirs = pl.pallas_call(
        halves_kernel,
        out_shape=[jax.ShapeDtypeStruct((2, CHANNELS, WIDTH), BF16)] * 2,
        in_specs=[vmem] * 2,
        out_specs=[vmem] * 2,
        compiler_params=pltpu.CompilerParams(vmem_limit_bytes=4 * 2**20),
        cost_estimate=pl.CostEstimate(flops=0, bytes_accessed=10**8, transcendentals=0),
    )(mine, theirs)
    theirs = lax.ppermute(theirs, BOTH, partners(CORE))
    stack = jnp.stack([mine, theirs], axis=1)
    stack = jnp.broadcast_to(stack.reshape(1, 2 * BLOCK, WIDTH), (SPOTS, 2 * BLOCK, WIDTH))
    tiles = lax.all_to_all(stack, BOTH, 0, 0, tiled=True, axis_index_groups=plane_groups)

    arrived = [lax.ppermute(messages[shift], BOTH, partners(shift)) for shift in (3, 2, 1)] + [messages[0]]
    arrived = jnp.stack(arrived)
    keep = lax.dynamic_slice_in_dim(arrived, core * SPAN, SPAN, 2)
    other = lax.dynamic_slice_in_dim(arrived[:, : 2 * PAIRS], (1 - core) * SPAN, SPAN, 2)

    code = tile_index.reshape(PAIRS, band) + TILES * tile_offset.reshape(PAIRS, band)
    other, code = lax.optimization_barrier((other, code))
    other = lax.ppermute(other, BOTH, partners(CORE))
    code = jnp.concatenate([code, lax.ppermute(code, BOTH, partners(CORE))], axis=0)
    index = (code & (TILES - 1)) ^ (view & 3)
    index = ((index >> 1) & 1) * 2 * SPOTS + (index & 1) * SPOTS + (index >> 2)
    code = index | (code & -TILES)

    wide = CHANNELS * DEPTH
    chosen, picks, bank = pl.pallas_call(
        prepare_kernel,
        out_shape=[
            jax.ShapeDtypeStruct((TILES, 128), F32),
            jax.ShapeDtypeStruct((2 * PAIRS, 2 * BANK * TILES), BF16),
            jax.ShapeDtypeStruct((BANK * DEPTH, WIDTH), BF16),
        ],
        in_specs=[vmem] * 2,
        out_specs=[vmem] * 3,
        scratch_shapes=[pltpu.VMEM((128, 128), F32)],
        compiler_params=pltpu.CompilerParams(vmem_limit_bytes=8 * 2**20),
    )(code, basis)
    rounded = call(
        forward_kernel,
        jax.ShapeDtypeStruct((2 * PAIRS, wide), BF16),
        FORWARD,
        picks,
        tiles,
        basis,
        keep,
        other,
    )
    swapped = lax.ppermute(rounded, BOTH, partners(CORE))
    total, power = call(
        own_kernel,
        [jax.ShapeDtypeStruct((CHANNELS * HALF, width), F32) for width in (WIDTH, 128)],
        BACKWARD,
        rounded,
        chosen,
        bank,
    )
    grads = call(
        other_kernel,
        jax.ShapeDtypeStruct((SPOTS, ROWS, 128), jnp.int16),
        BACKWARD + [pltpu.VMEM((SPOTS, ROWS, 128), F32)],
        swapped,
        chosen,
        bank,
        total,
        power,
    )

    parts = lax.all_to_all(grads, BOTH, 0, 0, tiled=True, axis_index_groups=plane_groups)
    scale = 1.0 / (8.0 * math.sqrt(views * lax.axis_size("view")))
    blocks = pl.pallas_call(
        functools.partial(sum_kernel, scale),
        out_shape=jax.ShapeDtypeStruct((2 * QUARTERS, BLOCK, WIDTH), F32),
        in_specs=[vmem],
        out_specs=vmem,
        compiler_params=pltpu.CompilerParams(vmem_limit_bytes=8 * 2**20),
    )(parts)
    blocks = lax.all_to_all(blocks, BOTH, 0, 0, tiled=True, axis_index_groups=line_groups)
    quarters = blocks[:4] + jnp.concatenate([blocks[6:], blocks[4:6]], axis=0)
    quarters = quarters.reshape(QUARTERS, 2, 3, 2, WIDTH).transpose(2, 0, 1, 3, 4)
    return quarters.reshape(1, 3, slices, WIDTH)


def solution(mesh):
    placed = (
        P("view", None, None, None),
        P(),
        P("view", None, None),
        P("view", None, None),
        P("bin", None),
        P("bin"),
        P("view", "bin", None, None),
    )
    return jax.shard_map(
        on_device,
        mesh=mesh,
        in_specs=placed,
        out_specs=P("view", None, None, None),
        check_vma=False,
    )
```
